32 devices in a mesh: blk: 4 (over y, core), ctx: 4 (over z), tp: 2 (over x).
Axes of the slice: x: 2, y: 2, z: 4, core: 2. Of those that a mesh axis runs over, the one named last changes fastest.
Arguments:
- query_proj: bfloat16 [2048, 4096], P(('blk', 'ctx'), 'tp'), may hold values from -6 to 6
- key_proj: bfloat16 [2048, 4096], P(('blk', 'ctx'), 'tp'), may hold values from -30 to 30
- value_proj: bfloat16 [2048, 4096], P(('blk', 'ctx'), 'tp'), may hold values from -6 to 6
- output_grad: bfloat16 [2048, 4096], P(('blk', 'ctx'), 'tp'), may hold values from -6 to 6
- long_filter: float32 [2, 2048, 2048], P('tp', ('blk', 'ctx')), may hold values from -0.6 to 0.6
Outputs:
- query_grad: bfloat16 [2048, 4096], P(('blk', 'ctx'), 'tp')
- key_grad: bfloat16 [2048, 4096], P(('blk', 'ctx'), 'tp')
- value_grad: bfloat16 [2048, 4096], P(('blk', 'ctx'), 'tp')
- filter_grad: float32 [2, 2048, 2048], P('tp', ('blk', 'ctx'))
The draws below stay inside these ranges and needn't reach their ends.
All inputs are finite; a program needn't handle non-finite values.
Results may differ from the reference program's by a relative error of at most 0.0085.
Values may be sent and summed in bfloat16 or wider, within the bound.
A program may use at most 128 MiB of HBM per device.

```python
import math
import jax
import jax.numpy as jnp
from jax import lax

D = 4096
LEN = 2048
CH_TP = 2048


def draw_key_proj(key, part):
    scale_key, jitter_key = jax.random.split(key, 2)
    channel = (jnp.arange(D) % CH_TP).astype(jnp.float32)
    rising = jnp.sqrt(1.0 + 2.0 * channel / max(CH_TP - 1, 1))
    spread = jnp.exp(math.log(10.0) * (jax.random.uniform(scale_key, (D,), jnp.float32) - 0.5))
    scales = 0.8 * rising * spread
    values = scales * jax.random.truncated_normal(jitter_key, -6.0, 6.0, (LEN, D), jnp.float32)
    return values.astype(jnp.bfloat16)


def draw_long_filter(key, part):
    rate_key, shape_key = jax.random.split(key, 2)
    decay = jnp.exp(jax.random.uniform(rate_key, (D // CH_TP, CH_TP, 1), jnp.float32, math.log(0.3), math.log(6.0)))
    position = jnp.arange(LEN, dtype=jnp.float32).reshape(1, 1, LEN) / LEN
    envelope = jnp.exp(-decay * position)
    norming = jnp.sqrt(2.0 * decay / (1.0 - jnp.exp(-2.0 * decay)) / LEN)
    shapes = jax.random.truncated_normal(shape_key, -6.0, 6.0, (D // CH_TP, CH_TP, LEN), jnp.float32)
    return (shapes * envelope * norming).astype(jnp.float32)


def shard_levels(rng, dims, cuts, least, top_value):
    loudness, own = 1.0, jax.random.fold_in(rng, 6)
    for dim, parts in cuts:
        steps = jnp.exp(jax.random.uniform(jax.random.fold_in(own, dim), (parts,), jnp.float32, least / len(cuts), top_value / len(cuts)))
        loudness = loudness * jnp.repeat(steps, dims[dim] // parts).reshape([-1 if axis == dim else 1 for axis in range(len(dims))])
    return loudness


def centred(own_key, dims, scale, most, cuts=(), kind=jnp.bfloat16):
    gain = shard_levels(own_key, dims, cuts, -0.22, 0.18) if cuts else 1.0
    result = jax.random.normal(own_key, dims, jnp.float32) * scale * gain
    return jnp.minimum(jnp.maximum(result, -most), most).astype(kind)


def setup_inputs(seed: int = 0) -> dict:
    arg_keys = jax.random.split(jax.random.key(seed), 6)
    return {
        "query_proj": centred(arg_keys[0], (LEN, D), 1.0, 6.0, ((0, 16), (1, 2))),
        "key_proj": draw_key_proj(jax.random.fold_in(arg_keys[5], 71), 0),
        "value_proj": centred(arg_keys[2], (LEN, D), 1.0, 6.0, ((0, 16), (1, 2))),
        "output_grad": centred(arg_keys[3], (LEN, D), 1.0, 6.0, ((0, 16), (1, 2))),
        "long_filter": draw_long_filter(jax.random.fold_in(arg_keys[5], 71), 0),
    }


def block_grads(pieces):
    gated, gate_part, kernel = pieces
    seq_length = gated.shape[-1]
    padded = 2 * seq_length
    gated_freq = jnp.fft.rfft(gated.astype(jnp.float32), n=padded, axis=-1)
    grad_freq = jnp.fft.rfft(gate_part.astype(jnp.float32), n=padded, axis=-1)
    kernel_freq = jnp.fft.rfft(kernel.astype(jnp.float32), n=padded, axis=-1)
    conv_out = jnp.fft.irfft(gated_freq * kernel_freq, n=padded, axis=-1)[:, :seq_length]
    conv_grad = jnp.fft.irfft(grad_freq * jnp.conj(kernel_freq), n=padded, axis=-1)[:, :seq_length]
    filter_raw = jnp.fft.irfft(grad_freq * jnp.conj(gated_freq), n=padded, axis=-1)[:, :seq_length]
    return (conv_out.astype(jnp.bfloat16), conv_grad.astype(jnp.bfloat16), filter_raw.astype(jnp.float32))

def reference(query_proj, key_proj, value_proj, output_grad, long_filter):
    key_value = (key_proj.astype(jnp.float32) * value_proj.astype(jnp.float32)).astype(jnp.bfloat16)
    gate_grad = (output_grad.astype(jnp.float32) * query_proj.astype(jnp.float32)).astype(jnp.bfloat16)
    group_rows = 256 if D % 256 == 0 else D
    blocks_count = D // group_rows
    kernel = long_filter.reshape(blocks_count, group_rows, LEN)
    stacked = (key_value.T.reshape(blocks_count, group_rows, LEN), gate_grad.T.reshape(blocks_count, group_rows, LEN), kernel)
    conv_out, conv_grad, filter_raw = lax.map(block_grads, stacked)
    conv_rows = conv_out.reshape(D, LEN).T
    grad_rows = conv_grad.reshape(D, LEN).T
    filter_raw = filter_raw.reshape(D, LEN)
    query_grad = (output_grad.astype(jnp.float32) * conv_rows.astype(jnp.float32)).astype(jnp.bfloat16)
    key_grad = (grad_rows.astype(jnp.float32) * value_proj.astype(jnp.float32)).astype(jnp.bfloat16)
    value_grad = (grad_rows.astype(jnp.float32) * key_proj.astype(jnp.float32)).astype(jnp.bfloat16)
    mean_square = jnp.sum(filter_raw * filter_raw) / (D * LEN)
    grad_rms = jnp.sqrt(mean_square + 1e-06)
    factor = jnp.minimum(1.0, 1.0 / grad_rms)
    filter_grad = (filter_raw * factor).reshape(D // CH_TP, CH_TP, LEN)
    return (query_grad, key_grad, value_grad, filter_grad)
```

```python
import functools
import math

import jax
import jax.numpy as jnp
import ml_dtypes
import numpy as np
from jax import lax
from jax.experimental import pallas as pl
from jax.experimental.pallas import tpu as pltpu
from jax.sharding import PartitionSpec as P

PRECISE = lax.Precision.HIGH
MESH = pl.DeviceIdType.MESH
TILE = 128
CHUNK = 16
F32 = jnp.float32
BF16 = jnp.bfloat16


def spectrum_tables(seq_length):
    outer_size = seq_length // 64
    half_size = outer_size // 2
    full_size = outer_size * 128
    row_index = lax.broadcasted_iota(jnp.int32, (outer_size, half_size), 0)
    col_index = lax.broadcasted_iota(jnp.int32, (outer_size, half_size), 1)
    outer_angle = (row_index * col_index % outer_size).astype(jnp.float32) * (
        2.0 * math.pi / outer_size
    )
    inner_row = lax.broadcasted_iota(jnp.int32, (128, 128), 0)
    inner_col = lax.broadcasted_iota(jnp.int32, (128, 128), 1)
    inner_angle = (inner_row * inner_col % 128).astype(jnp.float32) * (2.0 * math.pi / 128)
    twist_row = lax.broadcasted_iota(jnp.int32, (outer_size, 128), 0)
    twist_col = lax.broadcasted_iota(jnp.int32, (outer_size, 128), 1)
    twist_angle = (twist_row * twist_col % full_size).astype(jnp.float32) * (
        2.0 * math.pi / full_size
    )
    return (
        jnp.cos(outer_angle),
        jnp.sin(outer_angle),
        jnp.cos(inner_angle),
        jnp.sin(inner_angle),
        jnp.cos(twist_angle),
        jnp.sin(twist_angle),
        full_size,
    )


def to_spectrum(signal, tables):
    outer_cos, outer_sin, inner_cos, inner_sin, twist_cos, twist_sin, full_size = tables
    blocks = signal.reshape(signal.shape[0], outer_cos.shape[1], 128)
    first_real = jnp.einsum("kn,cnm->ckm", outer_cos, blocks, precision=PRECISE)
    first_imag = -jnp.einsum("kn,cnm->ckm", outer_sin, blocks, precision=PRECISE)
    turned_real = first_real * twist_cos + first_imag * twist_sin
    turned_imag = first_imag * twist_cos - first_real * twist_sin
    real_part = jnp.einsum("ckm,mj->ckj", turned_real, inner_cos, precision=PRECISE) + jnp.einsum(
        "ckm,mj->ckj", turned_imag, inner_sin, precision=PRECISE
    )
    imag_part = jnp.einsum("ckm,mj->ckj", turned_imag, inner_cos, precision=PRECISE) - jnp.einsum(
        "ckm,mj->ckj", turned_real, inner_sin, precision=PRECISE
    )
    return (real_part, imag_part)


def from_spectrum(spectrum, tables):
    outer_cos, outer_sin, inner_cos, inner_sin, twist_cos, twist_sin, full_size = tables
    real_part, imag_part = spectrum
    mixed_real = jnp.einsum("ckm,mj->ckj", real_part, inner_cos, precision=PRECISE) - jnp.einsum(
        "ckm,mj->ckj", imag_part, inner_sin, precision=PRECISE
    )
    mixed_imag = jnp.einsum("ckm,mj->ckj", imag_part, inner_cos, precision=PRECISE) + jnp.einsum(
        "ckm,mj->ckj", real_part, inner_sin, precision=PRECISE
    )
    turned_real = mixed_real * twist_cos - mixed_imag * twist_sin
    turned_imag = mixed_imag * twist_cos + mixed_real * twist_sin
    signal = jnp.einsum("kn,ckm->cnm", outer_cos, turned_real, precision=PRECISE) - jnp.einsum(
        "kn,ckm->cnm", outer_sin, turned_imag, precision=PRECISE
    )
    return (signal / full_size).reshape(signal.shape[0], -1)


def complex_product(left, right, conjugate):
    left_real, left_imag = left
    right_real, right_imag = right
    if conjugate:
        return (
            left_real * right_real + left_imag * right_imag,
            left_imag * right_real - left_real * right_imag,
        )
    return (
        left_real * right_real - left_imag * right_imag,
        left_real * right_imag + left_imag * right_real,
    )


def channel_work(gated_cols, gate_cols, kernel_cols):
    tables = spectrum_tables(kernel_cols.shape[1])
    kernel_spec = to_spectrum(kernel_cols, tables)
    gated_spec = to_spectrum(gated_cols.astype(jnp.float32), tables)
    gate_spec = to_spectrum(gate_cols.astype(jnp.float32), tables)
    conv_out = from_spectrum(complex_product(gated_spec, kernel_spec, False), tables).astype(
        jnp.bfloat16
    )
    conv_grad = from_spectrum(complex_product(gate_spec, kernel_spec, True), tables).astype(
        jnp.bfloat16
    )
    filter_raw = from_spectrum(complex_product(gate_spec, gated_spec, True), tables)
    return (conv_out, conv_grad, filter_raw)


def gated_product(left, right):
    return (left.astype(jnp.float32) * right.astype(jnp.float32)).astype(jnp.bfloat16)


def turn(value, step, span):
    re, im = value
    step = step % span
    if step == 0:
        return value
    if 4 * step == span:
        return (im, -re)
    if 2 * step == span:
        return (-re, -im)
    if 4 * step == 3 * span:
        return (-im, re)
    c = math.cos(2.0 * math.pi * step / span)
    s = math.sin(2.0 * math.pi * step / span)
    if (8 * step) % span == 0:
        r = abs(c)
        a, b = r * (re + im), r * (im - re)
        eighth = 8 * step // span
        return {1: (a, b), 3: (b, -a), 5: (-a, -b), 7: (-b, a)}[eighth]
    return (c * re + s * im, c * im - s * re)


def complex_dft(values, way):
    n = len(values)
    if n == 1:
        return values
    even = complex_dft(values[0::2], way)
    odd = complex_dft(values[1::2], way)
    out = [None] * n
    for k in range(n // 2):
        tr, ti = turn(odd[k], way * k, n)
        er, ei = even[k]
        out[k] = (er + tr, ei + ti)
        out[k + n // 2] = (er - tr, ei - ti)
    return out


def odd_bins(d, span):
    q = span // 4
    z = [turn((d[n], -d[n + q]), n, span) for n in range(q)]
    out = {}
    for m, (re, im) in enumerate(complex_dft(z, 1)):
        k = 4 * m + 1
        if k < span // 2:
            out[k] = (re, im)
        else:
            out[span - k] = (re, -im)
    return out


def real_bins(x):
    n = len(x)
    if n == 1:
        return {0: (x[0], None)}
    h = n // 2
    out = {2 * k: v for k, v in real_bins([x[i] + x[i + h] for i in range(h)]).items()}
    d = [x[i] - x[i + h] for i in range(h)]
    if n == 2:
        out[1] = (d[0], None)
    else:
        out.update(odd_bins(d, n))
    return out


def padded_bins(x):
    out = {2 * k: v for k, v in real_bins(x).items()}
    out.update(odd_bins(x, 2 * len(x)))
    return out


def odd_back(bins, span):
    q = span // 4
    c = []
    for m in range(q):
        k = 4 * m + 1
        if k < span // 2:
            c.append(bins[k])
        else:
            re, im = bins[span - k]
            c.append((re, -im))
    w = [turn(v, -n, span) for n, v in enumerate(complex_dft(c, -1))]
    return [v[0] for v in w] + [-v[1] for v in w]


def real_back(bins, n):
    if n == 1:
        return [bins[0][0]]
    if n == 2:
        return [bins[0][0] + bins[1][0], bins[0][0] - bins[1][0]]
    h = n // 2
    e = real_back({k // 2: bins[k] for k in bins if k % 2 == 0}, h)
    o = odd_back({k: bins[k] for k in bins if k % 2 == 1}, n)
    return [a + b for a, b in zip(e, o)] + [a - b for a, b in zip(e, o)]


def padded_back(bins, n):
    e = real_back({k // 2: bins[k] for k in bins if k % 2 == 0}, n)
    o = odd_back({k: bins[k] for k in bins if k % 2 == 1}, 2 * n)
    return [a + b for a, b in zip(e, o)]


def inner_tables(blocks):
    span = 2 * blocks
    full = span * TILE
    k1 = np.arange(blocks + 1).reshape(-1, 1, 1)
    k2 = np.arange(TILE).reshape(1, -1, 1)
    n2 = np.arange(TILE).reshape(1, 1, -1)
    angle = (n2 * (k1 + span * k2) % full) * (2.0 * math.pi / full)
    c, s = np.cos(angle), np.sin(angle)
    fwd = np.concatenate(
        [np.concatenate([c, s], 2), np.concatenate([-s, c], 2)], 1
    )
    weight = np.where((k1 == 0) | (k1 == blocks), 1.0, 2.0) / full
    inv = fwd.transpose(0, 2, 1) * weight

    def parts(m):
        hi = m.astype(ml_dtypes.bfloat16)
        lo = (m - hi.astype(np.float64)).astype(ml_dtypes.bfloat16)
        return np.concatenate([hi, lo], 1)

    return parts(fwd), parts(inv)


def fused_kernel(
    cfg,
    k_ref, v_ref, q_ref, og_ref, filt_ref, fwd_hbm, inv_hbm,
    co_ref, cg_ref, raw_ref, fac_ref,
    fwd, inv, send, recv, outer, spec_f, spec_kv, spec_gg, back, wide,
    sq_mine, sq_tp, sq_pair, sq_all,
    table_sem, send_sem, recv_sem, sq_send, sq_recv, tp_send, tp_recv,
):
    blocks, n_ctx, n_tp, entries = cfg
    me = lax.axis_index("blk") * n_ctx + lax.axis_index("ctx")
    my_tp = lax.axis_index("tp")
    bins = blocks + 1

    def place(d):
        return {"blk": d // n_ctx, "ctx": d % n_ctx}

    get_fwd = pltpu.make_async_copy(fwd_hbm, fwd, table_sem.at[0])
    get_inv = pltpu.make_async_copy(inv_hbm, inv, table_sem.at[1])
    get_fwd.start()
    get_inv.start()

    barrier = pltpu.get_barrier_semaphore()

    def greet(j, carry):
        d = lax.rem(me + j, blocks)
        pl.semaphore_signal(barrier, inc=1, device_id=place(d), device_id_type=MESH)
        return carry

    lax.fori_loop(1, blocks, greet, 0)
    for j in range(1, n_tp):
        pl.semaphore_signal(
            barrier, inc=1, device_id={"tp": lax.rem(my_tp + j, n_tp)}, device_id_type=MESH
        )

    def gate(phase, a_ref, b_ref):
        for d in range(blocks):
            cols = slice(d * TILE, (d + 1) * TILE)
            send[phase, d] = gated_product(a_ref[:, cols], b_ref[:, cols])
        recv[phase, me] = send[phase, me]

    def out_copy(phase, d):
        return pltpu.make_async_remote_copy(
            src_ref=send.at[phase, d],
            dst_ref=recv.at[phase, me],
            send_sem=send_sem.at[phase, d],
            recv_sem=recv_sem.at[phase, me],
            device_id=place(d),
            device_id_type=MESH,
        )

    def in_copy(phase, s):
        return pltpu.make_async_remote_copy(
            src_ref=send.at[phase, s],
            dst_ref=recv.at[phase, s],
            send_sem=send_sem.at[phase, s],
            recv_sem=recv_sem.at[phase, s],
            device_id=place(s),
            device_id_type=MESH,
        )

    def start_all(phase):
        def one(j, carry):
            out_copy(phase, lax.rem(me + j, blocks)).start()
            return carry

        lax.fori_loop(1, blocks, one, 0)

    def arrive_all(phase):
        def one(j, carry):
            in_copy(phase, lax.rem(me + blocks - j, blocks)).wait_recv()
            return carry

        lax.fori_loop(1, blocks, one, 0)

    def rows_at(i):
        return pl.ds(pl.multiple_of(i * CHUNK, CHUNK), CHUNK)

    def outer_forward(load):
        def one(i, carry):
            rows = rows_at(i)
            out = padded_bins([load(n, rows).astype(F32) for n in range(blocks)])
            low = pl.ds(pl.multiple_of(TILE + i * CHUNK, CHUNK), CHUNK)
            for k in range(bins):
                re, im = out[k]
                outer[k, rows, :] = re.astype(BF16)
                outer[k, low, :] = (jnp.zeros_like(re) if im is None else im).astype(BF16)
            return carry

        lax.fori_loop(0, TILE // CHUNK, one, 0)

    def apply(table, k, value):
        both = jnp.dot(table[k], value, preferred_element_type=F32)
        return both[: 2 * TILE] + both[2 * TILE :]

    def times(a, b, conjugate):
        ar, ai = a[:TILE], a[TILE:]
        br, bi = b[:TILE], b[TILE:]
        if conjugate:
            return jnp.concatenate([ar * br + ai * bi, ai * br - ar * bi], 0).astype(BF16)
        return jnp.concatenate([ar * br - ai * bi, ar * bi + ai * br], 0).astype(BF16)

    def outer_back(store):
        def one(i, carry):
            rows = rows_at(i)
            low = pl.ds(pl.multiple_of(TILE + i * CHUNK, CHUNK), CHUNK)
            got = {k: (back[k, rows, :], back[k, low, :]) for k in range(bins)}
            for n, y in enumerate(padded_back(got, blocks)):
                store(n, rows, y)
            return carry

        lax.fori_loop(0, TILE // CHUNK, one, 0)

    def store_send(phase):
        def store(n, rows, y):
            send[phase, n, rows, :] = y.astype(BF16)

        return store

    def store_wide(n, rows, y):
        wide[n, rows, :] = y

    gate(0, k_ref, v_ref)
    pl.semaphore_wait(barrier, blocks - 1 + n_tp - 1)
    start_all(0)
    gate(1, og_ref, q_ref)
    start_all(1)

    for n in range(blocks):
        wide[n] = filt_ref[:, n * TILE : (n + 1) * TILE].T
    outer_forward(lambda n, rows: wide[n, rows, :])
    get_fwd.wait()
    get_inv.wait()

    def filter_step(k, carry):
        spec_f[k] = apply(fwd, k, outer[k])
        return carry

    lax.fori_loop(0, bins, filter_step, 0)

    arrive_all(0)
    outer_forward(lambda n, rows: recv[0, n, rows, :])

    def gated_step(k, carry):
        spec = apply(fwd, k, outer[k])
        spec_kv[k] = spec
        back[k] = apply(inv, k, times(spec, spec_f[k], False))
        return carry

    lax.fori_loop(0, bins, gated_step, 0)
    outer_back(store_send(2))
    recv[2, me] = send[2, me]
    start_all(2)

    arrive_all(1)
    outer_forward(lambda n, rows: recv[1, n, rows, :])

    def gate_step(k, carry):
        spec = apply(fwd, k, outer[k])
        spec_gg[k] = spec
        back[k] = apply(inv, k, times(spec, spec_f[k], True))
        return carry

    lax.fori_loop(0, bins, gate_step, 0)
    outer_back(store_send(3))
    recv[3, me] = send[3, me]
    start_all(3)

    def raw_step(k, carry):
        back[k] = apply(inv, k, times(spec_gg[k], spec_kv[k], True))
        return carry

    lax.fori_loop(0, bins, raw_step, 0)
    outer_back(store_wide)
    total = jnp.zeros((8, TILE), F32)
    for n in range(blocks):
        tile = wide[n]
        raw_ref[:, n * TILE : (n + 1) * TILE] = tile.T
        total = total + jnp.sum((tile * tile).reshape(TILE // 8, 8, TILE), 0)
    sq_mine[...] = total

    def tp_copy(j):
        return pltpu.make_async_remote_copy(
            src_ref=sq_mine,
            dst_ref=sq_tp.at[j - 1],
            send_sem=tp_send.at[j - 1],
            recv_sem=tp_recv.at[j - 1],
            device_id={"tp": lax.rem(my_tp + j, n_tp)},
            device_id_type=MESH,
        )

    for j in range(1, n_tp):
        tp_copy(j).start()
    for j in range(1, n_tp):
        tp_copy(j).wait()
        total = total + sq_tp[j - 1]
    sq_pair[...] = total
    sq_all[me] = total

    def sq_out(d):
        return pltpu.make_async_remote_copy(
            src_ref=sq_pair,
            dst_ref=sq_all.at[me],
            send_sem=sq_send.at[d],
            recv_sem=sq_recv.at[me],
            device_id=place(d),
            device_id_type=MESH,
        )

    def sq_in(s):
        return pltpu.make_async_remote_copy(
            src_ref=sq_pair,
            dst_ref=sq_all.at[s],
            send_sem=sq_send.at[s],
            recv_sem=sq_recv.at[s],
            device_id=place(s),
            device_id_type=MESH,
        )

    def sq_start(j, carry):
        sq_out(lax.rem(me + j, blocks)).start()
        return carry

    def sq_arrive(j, carry):
        sq_in(lax.rem(me + blocks - j, blocks)).wait_recv()
        return carry

    lax.fori_loop(1, blocks, sq_start, 0)

    arrive_all(2)
    for s in range(blocks):
        co_ref[:, s * TILE : (s + 1) * TILE] = recv[2, s]
    lax.fori_loop(1, blocks, sq_arrive, 0)
    mean = jnp.sum(jnp.sum(sq_all[...], 0), keepdims=True) / entries
    rms = jnp.sqrt(mean + 1e-06)
    fac_ref[...] = jnp.broadcast_to(jnp.minimum(1.0, 1.0 / rms), (8, TILE))
    arrive_all(3)
    for s in range(blocks):
        cg_ref[:, s * TILE : (s + 1) * TILE] = recv[3, s]

    def sent(j, carry):
        d = lax.rem(me + j, blocks)
        for phase in range(4):
            out_copy(phase, d).wait_send()
        sq_out(d).wait_send()
        return carry

    lax.fori_loop(1, blocks, sent, 0)


def fused_body(mesh, query_proj, key_proj, value_proj, output_grad, long_filter):
    n_blk, n_ctx, n_tp = mesh.shape["blk"], mesh.shape["ctx"], mesh.shape["tp"]
    blocks = n_blk * n_ctx
    bins = blocks + 1
    tokens, width = query_proj.shape
    chan_count, seq_length = long_filter.shape[1:]
    entries = float(chan_count * seq_length * blocks * n_tp)
    fwd, inv = inner_tables(blocks)
    vmem = pl.BlockSpec(memory_space=pltpu.VMEM)
    hbm = pl.BlockSpec(memory_space=pl.ANY)
    dma = pltpu.SemaphoreType.DMA
    spec = pltpu.VMEM((bins, 2 * TILE, TILE), F32)
    flops = 6 * bins * 2 * 4 * TILE * 2 * TILE * TILE
    conv_out, conv_grad, filter_raw, factor = pl.pallas_call(
        functools.partial(fused_kernel, (blocks, n_ctx, n_tp, entries)),
        out_shape=(
            jax.ShapeDtypeStruct((tokens, width), BF16),
            jax.ShapeDtypeStruct((tokens, width), BF16),
            jax.ShapeDtypeStruct((chan_count, seq_length), F32),
            jax.ShapeDtypeStruct((8, TILE), F32),
        ),
        in_specs=[vmem] * 5 + [hbm] * 2,
        out_specs=(vmem,) * 4,
        scratch_shapes=[
            pltpu.VMEM(fwd.shape, BF16),
            pltpu.VMEM(inv.shape, BF16),
            pltpu.VMEM((4, blocks, TILE, TILE), BF16),
            pltpu.VMEM((4, blocks, TILE, TILE), BF16),
            pltpu.VMEM((bins, 2 * TILE, TILE), BF16),
            spec, spec, spec, spec,
            pltpu.VMEM((blocks, TILE, TILE), F32),
            pltpu.VMEM((8, TILE), F32),
            pltpu.VMEM((max(n_tp - 1, 1), 8, TILE), F32),
            pltpu.VMEM((8, TILE), F32),
            pltpu.VMEM((blocks, 8, TILE), F32),
            dma((2,)),
            dma((4, blocks)),
            dma((4, blocks)),
            dma((blocks,)),
            dma((blocks,)),
            dma((max(n_tp - 1, 1),)),
            dma((max(n_tp - 1, 1),)),
        ],
        compiler_params=pltpu.CompilerParams(
            collective_id=0, has_side_effects=True, vmem_limit_bytes=50 * 1024 * 1024
        ),
        cost_estimate=pl.CostEstimate(
            flops=flops, bytes_accessed=16 * tokens * width, transcendentals=0
        ),
    )(
        key_proj, value_proj, query_proj, output_grad,
        long_filter.reshape(chan_count, seq_length),
        jnp.asarray(fwd), jnp.asarray(inv),
    )
    query_grad = gated_product(output_grad, conv_out)
    key_grad = gated_product(conv_grad, value_proj)
    value_grad = gated_product(conv_grad, key_proj)
    filter_grad = (filter_raw * factor[0, 0]).reshape(1, chan_count, seq_length)
    return (query_grad, key_grad, value_grad, filter_grad)


def general_body(query_proj, key_proj, value_proj, output_grad, long_filter):
    axes = ("blk", "ctx")
    chan_count = long_filter.shape[1]
    seq_length = long_filter.shape[2]
    kernel_cols = long_filter.reshape(chan_count, seq_length)

    def to_channels(rows):
        return lax.all_to_all(rows.T, axes, split_axis=0, concat_axis=1, tiled=True)

    def to_tokens(cols):
        return lax.all_to_all(cols, axes, split_axis=1, concat_axis=0, tiled=True).T

    gated_cols = to_channels(gated_product(key_proj, value_proj))
    gate_cols = to_channels(gated_product(output_grad, query_proj))
    conv_out, conv_grad, filter_raw = channel_work(gated_cols, gate_cols, kernel_cols)
    conv_out, conv_grad = to_tokens(conv_out), to_tokens(conv_grad)
    query_grad = gated_product(output_grad, conv_out)
    key_grad = gated_product(conv_grad, value_proj)
    value_grad = gated_product(conv_grad, key_proj)
    square_total = lax.psum(jnp.sum(filter_raw * filter_raw), ("blk", "ctx", "tp"))
    entry_count = (
        chan_count * seq_length * lax.axis_size("blk") * lax.axis_size("ctx") * lax.axis_size("tp")
    )
    grad_rms = jnp.sqrt(square_total / entry_count + 1e-06)
    factor = jnp.minimum(1.0, 1.0 / grad_rms)
    filter_grad = (filter_raw * factor).reshape(1, chan_count, seq_length)
    return (query_grad, key_grad, value_grad, filter_grad)


def body(mesh, *args):
    blocks = mesh.shape["blk"] * mesh.shape["ctx"]
    fits = args[0].shape[0] == TILE and args[4].shape[1] == TILE and blocks in (4, 8, 16)
    if fits:
        return fused_body(mesh, *args)
    return general_body(*args)


def solution(mesh):
    in_specs = (
        P(("blk", "ctx"), "tp"),
        P(("blk", "ctx"), "tp"),
        P(("blk", "ctx"), "tp"),
        P(("blk", "ctx"), "tp"),
        P("tp", ("blk", "ctx"), None),
    )
    out_specs = (
        P(("blk", "ctx"), "tp"),
        P(("blk", "ctx"), "tp"),
        P(("blk", "ctx"), "tp"),
        P("tp", ("blk", "ctx"), None),
    )
    return jax.shard_map(
        functools.partial(body, mesh), mesh=mesh, in_specs=in_specs, out_specs=out_specs, check_vma=False
    )
```

```python
import functools
import math

import jax
import jax.numpy as jnp
import ml_dtypes
import numpy as np
from jax import lax
from jax.experimental import pallas as pl
from jax.experimental.pallas import tpu as pltpu
from jax.sharding import PartitionSpec as P

PRECISE = lax.Precision.HIGH
MESH = pl.DeviceIdType.MESH
TILE = 128
CHUNK = 16
GROUP = 2
F32 = jnp.float32
BF16 = jnp.bfloat16


def spectrum_tables(seq_length):
    outer_size = seq_length // 64
    half_size = outer_size // 2
    full_size = outer_size * 128
    row_index = lax.broadcasted_iota(jnp.int32, (outer_size, half_size), 0)
    col_index = lax.broadcasted_iota(jnp.int32, (outer_size, half_size), 1)
    outer_angle = (row_index * col_index % outer_size).astype(jnp.float32) * (
        2.0 * math.pi / outer_size
    )
    inner_row = lax.broadcasted_iota(jnp.int32, (128, 128), 0)
    inner_col = lax.broadcasted_iota(jnp.int32, (128, 128), 1)
    inner_angle = (inner_row * inner_col % 128).astype(jnp.float32) * (2.0 * math.pi / 128)
    twist_row = lax.broadcasted_iota(jnp.int32, (outer_size, 128), 0)
    twist_col = lax.broadcasted_iota(jnp.int32, (outer_size, 128), 1)
    twist_angle = (twist_row * twist_col % full_size).astype(jnp.float32) * (
        2.0 * math.pi / full_size
    )
    return (
        jnp.cos(outer_angle),
        jnp.sin(outer_angle),
        jnp.cos(inner_angle),
        jnp.sin(inner_angle),
        jnp.cos(twist_angle),
        jnp.sin(twist_angle),
        full_size,
    )


def to_spectrum(signal, tables):
    outer_cos, outer_sin, inner_cos, inner_sin, twist_cos, twist_sin, full_size = tables
    blocks = signal.reshape(signal.shape[0], outer_cos.shape[1], 128)
    first_real = jnp.einsum("kn,cnm->ckm", outer_cos, blocks, precision=PRECISE)
    first_imag = -jnp.einsum("kn,cnm->ckm", outer_sin, blocks, precision=PRECISE)
    turned_real = first_real * twist_cos + first_imag * twist_sin
    turned_imag = first_imag * twist_cos - first_real * twist_sin
    real_part = jnp.einsum("ckm,mj->ckj", turned_real, inner_cos, precision=PRECISE) + jnp.einsum(
        "ckm,mj->ckj", turned_imag, inner_sin, precision=PRECISE
    )
    imag_part = jnp.einsum("ckm,mj->ckj", turned_imag, inner_cos, precision=PRECISE) - jnp.einsum(
        "ckm,mj->ckj", turned_real, inner_sin, precision=PRECISE
    )
    return (real_part, imag_part)


def from_spectrum(spectrum, tables):
    outer_cos, outer_sin, inner_cos, inner_sin, twist_cos, twist_sin, full_size = tables
    real_part, imag_part = spectrum
    mixed_real = jnp.einsum("ckm,mj->ckj", real_part, inner_cos, precision=PRECISE) - jnp.einsum(
        "ckm,mj->ckj", imag_part, inner_sin, precision=PRECISE
    )
    mixed_imag = jnp.einsum("ckm,mj->ckj", imag_part, inner_cos, precision=PRECISE) + jnp.einsum(
        "ckm,mj->ckj", real_part, inner_sin, precision=PRECISE
    )
    turned_real = mixed_real * twist_cos - mixed_imag * twist_sin
    turned_imag = mixed_imag * twist_cos + mixed_real * twist_sin
    signal = jnp.einsum("kn,ckm->cnm", outer_cos, turned_real, precision=PRECISE) - jnp.einsum(
        "kn,ckm->cnm", outer_sin, turned_imag, precision=PRECISE
    )
    return (signal / full_size).reshape(signal.shape[0], -1)


def complex_product(left, right, conjugate):
    left_real, left_imag = left
    right_real, right_imag = right
    if conjugate:
        return (
            left_real * right_real + left_imag * right_imag,
            left_imag * right_real - left_real * right_imag,
        )
    return (
        left_real * right_real - left_imag * right_imag,
        left_real * right_imag + left_imag * right_real,
    )


def channel_work(gated_cols, gate_cols, kernel_cols):
    tables = spectrum_tables(kernel_cols.shape[1])
    kernel_spec = to_spectrum(kernel_cols, tables)
    gated_spec = to_spectrum(gated_cols.astype(jnp.float32), tables)
    gate_spec = to_spectrum(gate_cols.astype(jnp.float32), tables)
    conv_out = from_spectrum(complex_product(gated_spec, kernel_spec, False), tables).astype(
        jnp.bfloat16
    )
    conv_grad = from_spectrum(complex_product(gate_spec, kernel_spec, True), tables).astype(
        jnp.bfloat16
    )
    filter_raw = from_spectrum(complex_product(gate_spec, gated_spec, True), tables)
    return (conv_out, conv_grad, filter_raw)


def gated_product(left, right):
    return (left.astype(jnp.float32) * right.astype(jnp.float32)).astype(jnp.bfloat16)


def turn(value, step, span):
    re, im = value
    step = step % span
    if step == 0:
        return value
    if 4 * step == span:
        return (im, -re)
    if 2 * step == span:
        return (-re, -im)
    if 4 * step == 3 * span:
        return (-im, re)
    c = math.cos(2.0 * math.pi * step / span)
    s = math.sin(2.0 * math.pi * step / span)
    if (8 * step) % span == 0:
        r = abs(c)
        a, b = r * (re + im), r * (im - re)
        eighth = 8 * step // span
        return {1: (a, b), 3: (b, -a), 5: (-a, -b), 7: (-b, a)}[eighth]
    return (c * re + s * im, c * im - s * re)


def complex_dft(values, way):
    n = len(values)
    if n == 1:
        return values
    even = complex_dft(values[0::2], way)
    odd = complex_dft(values[1::2], way)
    out = [None] * n
    for k in range(n // 2):
        tr, ti = turn(odd[k], way * k, n)
        er, ei = even[k]
        out[k] = (er + tr, ei + ti)
        out[k + n // 2] = (er - tr, ei - ti)
    return out


def odd_bins(d, span):
    q = span // 4
    z = [turn((d[n], -d[n + q]), n, span) for n in range(q)]
    out = {}
    for m, (re, im) in enumerate(complex_dft(z, 1)):
        k = 4 * m + 1
        if k < span // 2:
            out[k] = (re, im)
        else:
            out[span - k] = (re, -im)
    return out


def real_bins(x):
    n = len(x)
    if n == 1:
        return {0: (x[0], None)}
    h = n // 2
    out = {2 * k: v for k, v in real_bins([x[i] + x[i + h] for i in range(h)]).items()}
    d = [x[i] - x[i + h] for i in range(h)]
    if n == 2:
        out[1] = (d[0], None)
    else:
        out.update(odd_bins(d, n))
    return out


def padded_bins(x):
    out = {2 * k: v for k, v in real_bins(x).items()}
    out.update(odd_bins(x, 2 * len(x)))
    return out


def odd_back(bins, span):
    q = span // 4
    c = []
    for m in range(q):
        k = 4 * m + 1
        if k < span // 2:
            c.append(bins[k])
        else:
            re, im = bins[span - k]
            c.append((re, -im))
    w = [turn(v, -n, span) for n, v in enumerate(complex_dft(c, -1))]
    return [v[0] for v in w] + [-v[1] for v in w]


def real_back(bins, n):
    if n == 1:
        return [bins[0][0]]
    if n == 2:
        return [bins[0][0] + bins[1][0], bins[0][0] - bins[1][0]]
    h = n // 2
    e = real_back({k // 2: bins[k] for k in bins if k % 2 == 0}, h)
    o = odd_back({k: bins[k] for k in bins if k % 2 == 1}, n)
    return [a + b for a, b in zip(e, o)] + [a - b for a, b in zip(e, o)]


def padded_back(bins, n):
    e = real_back({k // 2: bins[k] for k in bins if k % 2 == 0}, n)
    o = odd_back({k: bins[k] for k in bins if k % 2 == 1}, 2 * n)
    return [a + b for a, b in zip(e, o)]


def inner_tables(blocks):
    span = 2 * blocks
    full = span * TILE
    k1 = np.arange(blocks + 1).reshape(-1, 1, 1)
    k2 = np.arange(TILE).reshape(1, -1, 1)
    n2 = np.arange(TILE).reshape(1, 1, -1)
    angle = (n2 * (k1 + span * k2) % full) * (2.0 * math.pi / full)
    c, s = np.cos(angle), np.sin(angle)
    fwd = np.concatenate(
        [np.concatenate([c, s], 2), np.concatenate([-s, c], 2)], 1
    )
    weight = np.where((k1 == 0) | (k1 == blocks), 1.0, 2.0) / full
    inv = fwd.transpose(0, 2, 1) * weight

    return fwd.astype(ml_dtypes.bfloat16), inv.astype(ml_dtypes.bfloat16)


def fused_kernel(
    cfg,
    k_hbm, v_hbm, q_hbm, og_hbm, filt_hbm, fwd_hbm, inv_hbm,
    co_hbm, cg_hbm, raw_hbm, fac_ref,
    k_ref, v_ref, q_ref, og_ref, filt_ref, raw_ref, fwd, inv, send, recv, outer, spec_f, spec_kv, spec_gg, back, wide,
    sq_mine, sq_tp, sq_pair, sq_all,
    load_sem, store_sem, raw_sem, table_sem, send_sem, recv_sem, sq_send, sq_recv, tp_send, tp_recv,
):
    blocks, n_ctx, n_tp, entries = cfg
    me = lax.axis_index("blk") * n_ctx + lax.axis_index("ctx")
    my_tp = lax.axis_index("tp")
    bins = blocks + 1

    def place(d):
        return {"blk": d // n_ctx, "ctx": d % n_ctx}

    quarter = k_ref.shape[1] // 4

    def load(which, part):
        hbm, vmem = (
            (k_hbm, k_ref), (v_hbm, v_ref), (og_hbm, og_ref), (q_hbm, q_ref), (filt_hbm, filt_ref)
        )[which]
        cols = pl.ds(part * quarter, quarter)
        return pltpu.make_async_copy(
            hbm.at[:, cols], vmem.at[:, cols], load_sem.at[which, part]
        )

    for pair in ((0, 1), (2, 3), (4,)):
        for part in range(4):
            for which in pair:
                load(which, part).start()
    get_fwd = pltpu.make_async_copy(fwd_hbm, fwd, table_sem.at[0])
    get_inv = pltpu.make_async_copy(inv_hbm, inv, table_sem.at[1])
    get_fwd.start()
    get_inv.start()

    barrier = pltpu.get_barrier_semaphore()

    def greet(j, carry):
        d = lax.rem(me + j, blocks)
        pl.semaphore_signal(barrier, inc=1, device_id=place(d), device_id_type=MESH)
        return carry

    lax.fori_loop(1, blocks, greet, 0)
    for j in range(1, n_tp):
        pl.semaphore_signal(
            barrier, inc=1, device_id={"tp": lax.rem(my_tp + j, n_tp)}, device_id_type=MESH
        )

    def gate(phase, a_ref, b_ref):
        for d in range(blocks):
            if d % (blocks // 4) == 0:
                load(2 * phase, d // (blocks // 4)).wait()
                load(2 * phase + 1, d // (blocks // 4)).wait()
            cols = slice(d * TILE, (d + 1) * TILE)
            send[phase, d] = gated_product(a_ref[:, cols], b_ref[:, cols])
        recv[phase, me] = send[phase, me]

    def out_copy(phase, d):
        return pltpu.make_async_remote_copy(
            src_ref=send.at[phase, d],
            dst_ref=recv.at[phase, me],
            send_sem=send_sem.at[phase, d],
            recv_sem=recv_sem.at[phase, me],
            device_id=place(d),
            device_id_type=MESH,
        )

    def in_copy(phase, s):
        return pltpu.make_async_remote_copy(
            src_ref=send.at[phase, s],
            dst_ref=recv.at[phase, s],
            send_sem=send_sem.at[phase, s],
            recv_sem=recv_sem.at[phase, s],
            device_id=place(s),
            device_id_type=MESH,
        )

    def flipped(place_on_axis, mask):
        out, weight = 0, 1
        while weight < n_ctx:
            bit = lax.rem(place_on_axis // weight, 2)
            out = out + weight * (1 - bit if mask & weight else bit)
            weight *= 2
        return out

    def start_all(phase):
        for mask in range(n_ctx - 1, -1, -1):
            ctx = flipped(lax.axis_index("ctx"), mask)

            def one(j, carry, ctx=ctx):
                blk = lax.rem(lax.axis_index("blk") + j, blocks // n_ctx)
                out_copy(phase, blk * n_ctx + ctx).start()
                return carry

            lax.fori_loop(0 if mask else 1, blocks // n_ctx, one, 0)

    def arrive_all(phase):
        def one(j, carry):
            in_copy(phase, lax.rem(me + blocks - j, blocks)).wait_recv()
            return carry

        lax.fori_loop(1, blocks, one, 0)

    def rows_at(i):
        return pl.ds(pl.multiple_of(i * CHUNK, CHUNK), CHUNK)

    def outer_forward(load):
        def one(i, carry):
            rows = rows_at(i)
            out = padded_bins([load(n, rows).astype(F32) for n in range(blocks)])
            low = pl.ds(pl.multiple_of(TILE + i * CHUNK, CHUNK), CHUNK)
            for k in range(bins):
                re, im = out[k]
                outer[k, rows, :] = re.astype(BF16)
                outer[k, low, :] = (jnp.zeros_like(re) if im is None else im).astype(BF16)
            return carry

        lax.fori_loop(0, TILE // CHUNK, one, 0)

    def apply(table, k, value):
        return jnp.dot(table[k], value, preferred_element_type=F32)

    def times(a, b, conjugate):
        ar, ai = a[:TILE], a[TILE:]
        br, bi = b[:TILE], b[TILE:]
        if conjugate:
            return jnp.concatenate([ar * br + ai * bi, ai * br - ar * bi], 0).astype(BF16)
        return jnp.concatenate([ar * br - ai * bi, ar * bi + ai * br], 0).astype(BF16)

    def outer_back(store):
        def one(i, carry):
            rows = rows_at(i)
            low = pl.ds(pl.multiple_of(TILE + i * CHUNK, CHUNK), CHUNK)
            got = {k: (back[k, rows, :], back[k, low, :]) for k in range(bins)}
            for n, y in enumerate(padded_back(got, blocks)):
                store(n, rows, y)
            return carry

        lax.fori_loop(0, TILE // CHUNK, one, 0)

    def store_send(phase):
        def store(n, rows, y):
            send[phase, n, rows, :] = y.astype(BF16)

        return store

    def store_wide(n, rows, y):
        wide[n, rows, :] = y

    gate(0, k_ref, v_ref)
    pl.semaphore_wait(barrier, blocks - 1 + n_tp - 1)
    start_all(0)
    gate(1, og_ref, q_ref)
    start_all(1)

    for part in range(4):
        load(4, part).wait()
    for n in range(blocks):
        wide[n] = filt_ref[:, n * TILE : (n + 1) * TILE].T
    outer_forward(lambda n, rows: wide[n, rows, :])
    get_fwd.wait()
    get_inv.wait()

    def each_bin(step):
        def group(i, carry):
            step([GROUP * i + g for g in range(GROUP)])
            return carry

        lax.fori_loop(0, bins // GROUP, group, 0)
        if bins % GROUP:
            step(list(range(bins - bins % GROUP, bins)))

    def filter_step(ks):
        specs = [apply(fwd, k, outer[k]) for k in ks]
        for k, spec in zip(ks, specs):
            spec_f[k] = spec

    each_bin(filter_step)

    arrive_all(0)
    outer_forward(lambda n, rows: recv[0, n, rows, :])

    def gated_step(ks):
        specs = [apply(fwd, k, outer[k]) for k in ks]
        products = [times(spec, spec_f[k], False) for k, spec in zip(ks, specs)]
        results = [apply(inv, k, product) for k, product in zip(ks, products)]
        for k, spec, result in zip(ks, specs, results):
            spec_kv[k] = spec
            back[k] = result

    each_bin(gated_step)
    outer_back(store_send(2))
    recv[2, me] = send[2, me]
    start_all(2)

    arrive_all(1)
    outer_forward(lambda n, rows: recv[1, n, rows, :])

    def gate_step(ks):
        specs = [apply(fwd, k, outer[k]) for k in ks]
        products = [times(spec, spec_f[k], True) for k, spec in zip(ks, specs)]
        results = [apply(inv, k, product) for k, product in zip(ks, products)]
        for k, spec, result in zip(ks, specs, results):
            spec_gg[k] = spec
            back[k] = result

    each_bin(gate_step)
    outer_back(store_send(3))
    recv[3, me] = send[3, me]
    start_all(3)

    def raw_step(ks):
        products = [times(spec_gg[k], spec_kv[k], True) for k in ks]
        results = [apply(inv, k, product) for k, product in zip(ks, products)]
        for k, result in zip(ks, results):
            back[k] = result

    each_bin(raw_step)
    outer_back(store_wide)
    total = jnp.zeros((8, TILE), F32)
    for n in range(blocks):
        tile = wide[n]
        raw_ref[:, n * TILE : (n + 1) * TILE] = tile.T
        total = total + jnp.sum((tile * tile).reshape(TILE // 8, 8, TILE), 0)
    put_raw = pltpu.make_async_copy(raw_ref, raw_hbm, raw_sem)
    put_raw.start()
    sq_mine[...] = total

    def tp_copy(j):
        return pltpu.make_async_remote_copy(
            src_ref=sq_mine,
            dst_ref=sq_tp.at[j - 1],
            send_sem=tp_send.at[j - 1],
            recv_sem=tp_recv.at[j - 1],
            device_id={"tp": lax.rem(my_tp + j, n_tp)},
            device_id_type=MESH,
        )

    for j in range(1, n_tp):
        tp_copy(j).start()
    for j in range(1, n_tp):
        tp_copy(j).wait()
        total = total + sq_tp[j - 1]
    sq_pair[...] = total
    sq_all[me] = total

    def sq_out(d):
        return pltpu.make_async_remote_copy(
            src_ref=sq_pair,
            dst_ref=sq_all.at[me],
            send_sem=sq_send.at[d],
            recv_sem=sq_recv.at[me],
            device_id=place(d),
            device_id_type=MESH,
        )

    def sq_in(s):
        return pltpu.make_async_remote_copy(
            src_ref=sq_pair,
            dst_ref=sq_all.at[s],
            send_sem=sq_send.at[s],
            recv_sem=sq_recv.at[s],
            device_id=place(s),
            device_id_type=MESH,
        )

    def sq_start(j, carry):
        sq_out(lax.rem(me + j, blocks)).start()
        return carry

    def sq_arrive(j, carry):
        sq_in(lax.rem(me + blocks - j, blocks)).wait_recv()
        return carry

    lax.fori_loop(1, blocks, sq_start, 0)

    def put(phase, hbm, s):
        return pltpu.make_async_copy(
            recv.at[phase, s],
            hbm.at[:, pl.ds(pl.multiple_of(s * TILE, TILE), TILE)],
            store_sem.at[phase - 2, s],
        )

    def put_all(phase, hbm):
        put(phase, hbm, me).start()

        def one(j, carry):
            s = lax.rem(me + blocks - j, blocks)
            in_copy(phase, s).wait_recv()
            put(phase, hbm, s).start()
            return carry

        lax.fori_loop(1, blocks, one, 0)

    put_all(2, co_hbm)
    lax.fori_loop(1, blocks, sq_arrive, 0)
    mean = jnp.sum(jnp.sum(sq_all[...], 0), keepdims=True) / entries
    rms = jnp.sqrt(mean + 1e-06)
    fac_ref[...] = jnp.minimum(1.0, 1.0 / rms)
    put_all(3, cg_hbm)

    def stored(s, carry):
        put(2, co_hbm, s).wait()
        put(3, cg_hbm, s).wait()
        return carry

    def sent(j, carry):
        d = lax.rem(me + j, blocks)
        for phase in range(4):
            out_copy(phase, d).wait_send()
        sq_out(d).wait_send()
        return carry

    lax.fori_loop(1, blocks, sent, 0)
    put_raw.wait()
    lax.fori_loop(0, blocks, stored, 0)


def fused_body(mesh, query_proj, key_proj, value_proj, output_grad, long_filter):
    n_blk, n_ctx, n_tp = mesh.shape["blk"], mesh.shape["ctx"], mesh.shape["tp"]
    blocks = n_blk * n_ctx
    bins = blocks + 1
    tokens, width = query_proj.shape
    chan_count, seq_length = long_filter.shape[1:]
    entries = float(chan_count * seq_length * blocks * n_tp)
    fwd, inv = inner_tables(blocks)
    vmem = pl.BlockSpec(memory_space=pltpu.VMEM)
    hbm = pl.BlockSpec(memory_space=pltpu.HBM)
    stream = pltpu.VMEM((tokens, width), BF16)
    lags = pltpu.VMEM((chan_count, seq_length), F32)
    dma = pltpu.SemaphoreType.DMA
    spec = pltpu.VMEM((bins, 2 * TILE, TILE), F32)
    flops = 6 * bins * 2 * 2 * TILE * 2 * TILE * TILE
    conv_out, conv_grad, filter_raw, factor = pl.pallas_call(
        functools.partial(fused_kernel, (blocks, n_ctx, n_tp, entries)),
        out_shape=(
            jax.ShapeDtypeStruct((tokens, width), BF16),
            jax.ShapeDtypeStruct((tokens, width), BF16),
            jax.ShapeDtypeStruct((chan_count, seq_length), F32),
            jax.ShapeDtypeStruct((1, 1), F32),
        ),
        in_specs=[hbm] * 7,
        out_specs=(hbm, hbm, hbm, vmem),
        scratch_shapes=[
            stream, stream, stream, stream, lags, lags,
            pltpu.VMEM(fwd.shape, BF16),
            pltpu.VMEM(inv.shape, BF16),
            pltpu.VMEM((4, blocks, TILE, TILE), BF16),
            pltpu.VMEM((4, blocks, TILE, TILE), BF16),
            pltpu.VMEM((bins, 2 * TILE, TILE), BF16),
            spec, spec, spec, spec,
            pltpu.VMEM((blocks, TILE, TILE), F32),
            pltpu.VMEM((8, TILE), F32),
            pltpu.VMEM((max(n_tp - 1, 1), 8, TILE), F32),
            pltpu.VMEM((8, TILE), F32),
            pltpu.VMEM((blocks, 8, TILE), F32),
            dma((5, 4)),
            dma((2, blocks)),
            dma(()),
            dma((2,)),
            dma((4, blocks)),
            dma((4, blocks)),
            dma((blocks,)),
            dma((blocks,)),
            dma((max(n_tp - 1, 1),)),
            dma((max(n_tp - 1, 1),)),
        ],
        compiler_params=pltpu.CompilerParams(
            collective_id=0, has_side_effects=True, vmem_limit_bytes=50 * 1024 * 1024
        ),
        cost_estimate=pl.CostEstimate(
            flops=flops, bytes_accessed=16 * tokens * width, transcendentals=0
        ),
    )(
        key_proj, value_proj, query_proj, output_grad,
        long_filter.reshape(chan_count, seq_length),
        jnp.asarray(fwd), jnp.asarray(inv),
    )
    query_grad = gated_product(output_grad, conv_out)
    key_grad = gated_product(conv_grad, value_proj)
    value_grad = gated_product(conv_grad, key_proj)
    filter_grad = (filter_raw * factor.reshape(())).reshape(1, chan_count, seq_length)
    return (query_grad, key_grad, value_grad, filter_grad)


def general_body(query_proj, key_proj, value_proj, output_grad, long_filter):
    axes = ("blk", "ctx")
    chan_count = long_filter.shape[1]
    seq_length = long_filter.shape[2]
    kernel_cols = long_filter.reshape(chan_count, seq_length)

    def to_channels(rows):
        return lax.all_to_all(rows.T, axes, split_axis=0, concat_axis=1, tiled=True)

    def to_tokens(cols):
        return lax.all_to_all(cols, axes, split_axis=1, concat_axis=0, tiled=True).T

    gated_cols = to_channels(gated_product(key_proj, value_proj))
    gate_cols = to_channels(gated_product(output_grad, query_proj))
    conv_out, conv_grad, filter_raw = channel_work(gated_cols, gate_cols, kernel_cols)
    conv_out, conv_grad = to_tokens(conv_out), to_tokens(conv_grad)
    query_grad = gated_product(output_grad, conv_out)
    key_grad = gated_product(conv_grad, value_proj)
    value_grad = gated_product(conv_grad, key_proj)
    square_total = lax.psum(jnp.sum(filter_raw * filter_raw), ("blk", "ctx", "tp"))
    entry_count = (
        chan_count * seq_length * lax.axis_size("blk") * lax.axis_size("ctx") * lax.axis_size("tp")
    )
    grad_rms = jnp.sqrt(square_total / entry_count + 1e-06)
    factor = jnp.minimum(1.0, 1.0 / grad_rms)
    filter_grad = (filter_raw * factor).reshape(1, chan_count, seq_length)
    return (query_grad, key_grad, value_grad, filter_grad)


def body(mesh, *args):
    blocks = mesh.shape["blk"] * mesh.shape["ctx"]
    fits = args[0].shape[0] == TILE and args[4].shape[1] == TILE and blocks in (4, 8, 16)
    if fits:
        return fused_body(mesh, *args)
    return general_body(*args)


def solution(mesh):
    in_specs = (
        P(("blk", "ctx"), "tp"),
        P(("blk", "ctx"), "tp"),
        P(("blk", "ctx"), "tp"),
        P(("blk", "ctx"), "tp"),
        P("tp", ("blk", "ctx"), None),
    )
    out_specs = (
        P(("blk", "ctx"), "tp"),
        P(("blk", "ctx"), "tp"),
        P(("blk", "ctx"), "tp"),
        P("tp", ("blk", "ctx"), None),
    )
    return jax.shard_map(
        functools.partial(body, mesh), mesh=mesh, in_specs=in_specs, out_specs=out_specs, check_vma=False
    )
```

```python
import functools
import math

import jax
import jax.numpy as jnp
import ml_dtypes
import numpy as np
from jax import lax
from jax.experimental import pallas as pl
from jax.experimental.pallas import tpu as pltpu
from jax.sharding import PartitionSpec as P

PRECISE = lax.Precision.HIGH
MESH = pl.DeviceIdType.MESH
TILE = 128
PARTS = 4
CHUNK = 16
GROUP = 4
VMEM_LIMIT = 63 * 1024 * 1024
F32 = jnp.float32
BF16 = jnp.bfloat16


def spectrum_tables(seq_length):
    outer_size = seq_length // 64
    half_size = outer_size // 2
    full_size = outer_size * 128
    row_index = lax.broadcasted_iota(jnp.int32, (outer_size, half_size), 0)
    col_index = lax.broadcasted_iota(jnp.int32, (outer_size, half_size), 1)
    outer_angle = (row_index * col_index % outer_size).astype(jnp.float32) * (
        2.0 * math.pi / outer_size
    )
    inner_row = lax.broadcasted_iota(jnp.int32, (128, 128), 0)
    inner_col = lax.broadcasted_iota(jnp.int32, (128, 128), 1)
    inner_angle = (inner_row * inner_col % 128).astype(jnp.float32) * (2.0 * math.pi / 128)
    twist_row = lax.broadcasted_iota(jnp.int32, (outer_size, 128), 0)
    twist_col = lax.broadcasted_iota(jnp.int32, (outer_size, 128), 1)
    twist_angle = (twist_row * twist_col % full_size).astype(jnp.float32) * (
        2.0 * math.pi / full_size
    )
    return (
        jnp.cos(outer_angle),
        jnp.sin(outer_angle),
        jnp.cos(inner_angle),
        jnp.sin(inner_angle),
        jnp.cos(twist_angle),
        jnp.sin(twist_angle),
        full_size,
    )


def to_spectrum(signal, tables):
    outer_cos, outer_sin, inner_cos, inner_sin, twist_cos, twist_sin, full_size = tables
    blocks = signal.reshape(signal.shape[0], outer_cos.shape[1], 128)
    first_real = jnp.einsum("kn,cnm->ckm", outer_cos, blocks, precision=PRECISE)
    first_imag = -jnp.einsum("kn,cnm->ckm", outer_sin, blocks, precision=PRECISE)
    turned_real = first_real * twist_cos + first_imag * twist_sin
    turned_imag = first_imag * twist_cos - first_real * twist_sin
    real_part = jnp.einsum("ckm,mj->ckj", turned_real, inner_cos, precision=PRECISE) + jnp.einsum(
        "ckm,mj->ckj", turned_imag, inner_sin, precision=PRECISE
    )
    imag_part = jnp.einsum("ckm,mj->ckj", turned_imag, inner_cos, precision=PRECISE) - jnp.einsum(
        "ckm,mj->ckj", turned_real, inner_sin, precision=PRECISE
    )
    return (real_part, imag_part)


def from_spectrum(spectrum, tables):
    outer_cos, outer_sin, inner_cos, inner_sin, twist_cos, twist_sin, full_size = tables
    real_part, imag_part = spectrum
    mixed_real = jnp.einsum("ckm,mj->ckj", real_part, inner_cos, precision=PRECISE) - jnp.einsum(
        "ckm,mj->ckj", imag_part, inner_sin, precision=PRECISE
    )
    mixed_imag = jnp.einsum("ckm,mj->ckj", imag_part, inner_cos, precision=PRECISE) + jnp.einsum(
        "ckm,mj->ckj", real_part, inner_sin, precision=PRECISE
    )
    turned_real = mixed_real * twist_cos - mixed_imag * twist_sin
    turned_imag = mixed_imag * twist_cos + mixed_real * twist_sin
    signal = jnp.einsum("kn,ckm->cnm", outer_cos, turned_real, precision=PRECISE) - jnp.einsum(
        "kn,ckm->cnm", outer_sin, turned_imag, precision=PRECISE
    )
    return (signal / full_size).reshape(signal.shape[0], -1)


def complex_product(left, right, conjugate):
    left_real, left_imag = left
    right_real, right_imag = right
    if conjugate:
        return (
            left_real * right_real + left_imag * right_imag,
            left_imag * right_real - left_real * right_imag,
        )
    return (
        left_real * right_real - left_imag * right_imag,
        left_real * right_imag + left_imag * right_real,
    )


def channel_work(gated_cols, gate_cols, kernel_cols):
    tables = spectrum_tables(kernel_cols.shape[1])
    kernel_spec = to_spectrum(kernel_cols, tables)
    gated_spec = to_spectrum(gated_cols.astype(jnp.float32), tables)
    gate_spec = to_spectrum(gate_cols.astype(jnp.float32), tables)
    conv_out = from_spectrum(complex_product(gated_spec, kernel_spec, False), tables).astype(
        jnp.bfloat16
    )
    conv_grad = from_spectrum(complex_product(gate_spec, kernel_spec, True), tables).astype(
        jnp.bfloat16
    )
    filter_raw = from_spectrum(complex_product(gate_spec, gated_spec, True), tables)
    return (conv_out, conv_grad, filter_raw)


def gated_product(left, right):
    return (left.astype(jnp.float32) * right.astype(jnp.float32)).astype(jnp.bfloat16)


def turn(value, step, span):
    re, im = value
    step = step % span
    if step == 0:
        return value
    if 4 * step == span:
        return (im, -re)
    if 2 * step == span:
        return (-re, -im)
    if 4 * step == 3 * span:
        return (-im, re)
    c = math.cos(2.0 * math.pi * step / span)
    s = math.sin(2.0 * math.pi * step / span)
    if (8 * step) % span == 0:
        r = abs(c)
        a, b = r * (re + im), r * (im - re)
        eighth = 8 * step // span
        return {1: (a, b), 3: (b, -a), 5: (-a, -b), 7: (-b, a)}[eighth]
    return (c * re + s * im, c * im - s * re)


def complex_dft(values, way):
    n = len(values)
    if n == 1:
        return values
    even = complex_dft(values[0::2], way)
    odd = complex_dft(values[1::2], way)
    out = [None] * n
    for k in range(n // 2):
        tr, ti = turn(odd[k], way * k, n)
        er, ei = even[k]
        out[k] = (er + tr, ei + ti)
        out[k + n // 2] = (er - tr, ei - ti)
    return out


def odd_bins(d, span):
    q = span // 4
    z = [turn((d[n], -d[n + q]), n, span) for n in range(q)]
    out = {}
    for m, (re, im) in enumerate(complex_dft(z, 1)):
        k = 4 * m + 1
        if k < span // 2:
            out[k] = (re, im)
        else:
            out[span - k] = (re, -im)
    return out


def real_bins(x):
    n = len(x)
    if n == 1:
        return {0: (x[0], None)}
    h = n // 2
    out = {2 * k: v for k, v in real_bins([x[i] + x[i + h] for i in range(h)]).items()}
    d = [x[i] - x[i + h] for i in range(h)]
    if n == 2:
        out[1] = (d[0], None)
    else:
        out.update(odd_bins(d, n))
    return out


def padded_bins(x):
    out = {2 * k: v for k, v in real_bins(x).items()}
    out.update(odd_bins(x, 2 * len(x)))
    return out


def odd_back(bins, span):
    q = span // 4
    c = []
    for m in range(q):
        k = 4 * m + 1
        if k < span // 2:
            c.append(bins[k])
        else:
            re, im = bins[span - k]
            c.append((re, -im))
    w = [turn(v, -n, span) for n, v in enumerate(complex_dft(c, -1))]
    return [v[0] for v in w] + [-v[1] for v in w]


def real_back(bins, n):
    if n == 1:
        return [bins[0][0]]
    if n == 2:
        return [bins[0][0] + bins[1][0], bins[0][0] - bins[1][0]]
    h = n // 2
    e = real_back({k // 2: bins[k] for k in bins if k % 2 == 0}, h)
    o = odd_back({k: bins[k] for k in bins if k % 2 == 1}, n)
    return [a + b for a, b in zip(e, o)] + [a - b for a, b in zip(e, o)]


def padded_back(bins, n):
    e = real_back({k // 2: bins[k] for k in bins if k % 2 == 0}, n)
    o = odd_back({k: bins[k] for k in bins if k % 2 == 1}, 2 * n)
    return [a + b for a, b in zip(e, o)]


def inner_tables(blocks):
    span = 2 * blocks
    full = span * TILE
    k1 = np.arange(blocks + 1).reshape(-1, 1, 1)
    k2 = np.arange(TILE).reshape(1, -1, 1)
    n2 = np.arange(TILE).reshape(1, 1, -1)
    angle = (n2 * (k1 + span * k2) % full) * (2.0 * math.pi / full)
    c, s = np.cos(angle), np.sin(angle)
    fwd = np.concatenate(
        [np.concatenate([c, s], 2), np.concatenate([-s, c], 2)], 1
    )
    weight = np.where((k1 == 0) | (k1 == blocks), 1.0, 2.0) / full
    inv = fwd.transpose(0, 2, 1) * weight

    return fwd.astype(ml_dtypes.bfloat16), inv.astype(ml_dtypes.bfloat16)


def fused_kernel(
    cfg,
    k_hbm, v_hbm, q_hbm, og_hbm, filt_hbm, fwd_hbm, inv_hbm,
    co_hbm, cg_hbm, raw_hbm, fac_ref,
    k_ref, v_ref, q_ref, og_ref, filt_ref, raw_ref, fwd, inv, send, recv, outer, spec_f, spec_kv, spec_gg, back, wide,
    sq_mine, sq_tp, sq_pair, sq_all,
    load_sem, store_sem, raw_sem, table_sem, send_sem, recv_sem, sq_send, sq_recv, tp_send, tp_recv,
):
    blocks, n_ctx, n_tp, entries = cfg
    me = lax.axis_index("blk") * n_ctx + lax.axis_index("ctx")
    my_tp = lax.axis_index("tp")
    bins = blocks + 1

    def place(d):
        return {"blk": d // n_ctx, "ctx": d % n_ctx}

    quarter = k_ref.shape[1] // 4

    def load(which, part):
        hbm, vmem = (
            (k_hbm, k_ref), (v_hbm, v_ref), (og_hbm, og_ref), (q_hbm, q_ref), (filt_hbm, filt_ref)
        )[which]
        cols = pl.ds(part * quarter, quarter)
        return pltpu.make_async_copy(
            hbm.at[:, cols], vmem.at[:, cols], load_sem.at[which, part]
        )

    for pair in ((0, 1), (2, 3), (4,)):
        for part in range(4):
            for which in pair:
                load(which, part).start()
    get_fwd = pltpu.make_async_copy(fwd_hbm, fwd, table_sem.at[0])
    get_inv = pltpu.make_async_copy(inv_hbm, inv, table_sem.at[1])
    get_fwd.start()
    get_inv.start()

    barrier = pltpu.get_barrier_semaphore()

    def greet(j, carry):
        d = lax.rem(me + j, blocks)
        pl.semaphore_signal(barrier, inc=1, device_id=place(d), device_id_type=MESH)
        return carry

    lax.fori_loop(1, blocks, greet, 0)
    for j in range(1, n_tp):
        pl.semaphore_signal(
            barrier, inc=1, device_id={"tp": lax.rem(my_tp + j, n_tp)}, device_id_type=MESH
        )

    def gate(phase, a_ref, b_ref):
        for d in range(blocks):
            if d % (blocks // 4) == 0:
                load(2 * phase, d // (blocks // 4)).wait()
                load(2 * phase + 1, d // (blocks // 4)).wait()
            cols = slice(d * TILE, (d + 1) * TILE)
            send[phase, d] = gated_product(a_ref[:, cols], b_ref[:, cols])
        recv[phase, me] = send[phase, me]

    def out_copy(phase, d):
        return pltpu.make_async_remote_copy(
            src_ref=send.at[phase, d],
            dst_ref=recv.at[phase, me],
            send_sem=send_sem.at[phase, d],
            recv_sem=recv_sem.at[phase, me],
            device_id=place(d),
            device_id_type=MESH,
        )

    def in_copy(phase, s):
        return pltpu.make_async_remote_copy(
            src_ref=send.at[phase, s],
            dst_ref=recv.at[phase, s],
            send_sem=send_sem.at[phase, s],
            recv_sem=recv_sem.at[phase, s],
            device_id=place(s),
            device_id_type=MESH,
        )

    def flipped(place_on_axis, mask):
        out, weight = 0, 1
        while weight < n_ctx:
            bit = lax.rem(place_on_axis // weight, 2)
            out = out + weight * (1 - bit if mask & weight else bit)
            weight *= 2
        return out

    def start_all(phase):
        for mask in range(n_ctx - 1, -1, -1):
            ctx = flipped(lax.axis_index("ctx"), mask)

            def one(j, carry, ctx=ctx):
                blk = lax.rem(lax.axis_index("blk") + j, blocks // n_ctx)
                out_copy(phase, blk * n_ctx + ctx).start()
                return carry

            lax.fori_loop(0 if mask else 1, blocks // n_ctx, one, 0)

    def arrive_all(phase):
        def one(j, carry):
            in_copy(phase, lax.rem(me + blocks - j, blocks)).wait_recv()
            return carry

        lax.fori_loop(1, blocks, one, 0)

    def rows_at(i):
        return pl.ds(pl.multiple_of(i * CHUNK, CHUNK), CHUNK)

    def outer_forward(load):
        def one(i, carry):
            rows = rows_at(i)
            out = padded_bins([load(n, rows).astype(F32) for n in range(blocks)])
            low = pl.ds(pl.multiple_of(TILE + i * CHUNK, CHUNK), CHUNK)
            for k in range(bins):
                re, im = out[k]
                outer[k, rows, :] = re.astype(BF16)
                outer[k, low, :] = (jnp.zeros_like(re) if im is None else im).astype(BF16)
            return carry

        lax.fori_loop(0, TILE // CHUNK, one, 0)

    def apply(table, k, value):
        return jnp.dot(table[k], value, preferred_element_type=F32)

    def times(a, b, conjugate):
        ar, ai = a[:TILE], a[TILE:]
        br, bi = b[:TILE], b[TILE:]
        if conjugate:
            return jnp.concatenate([ar * br + ai * bi, ai * br - ar * bi], 0).astype(BF16)
        return jnp.concatenate([ar * br - ai * bi, ar * bi + ai * br], 0).astype(BF16)

    def outer_back(store):
        def one(i, carry):
            rows = rows_at(i)
            low = pl.ds(pl.multiple_of(TILE + i * CHUNK, CHUNK), CHUNK)
            got = {k: (back[k, rows, :], back[k, low, :]) for k in range(bins)}
            for n, y in enumerate(padded_back(got, blocks)):
                store(n, rows, y)
            return carry

        lax.fori_loop(0, TILE // CHUNK, one, 0)

    def store_send(phase):
        def store(n, rows, y):
            send[phase, n, rows, :] = y.astype(BF16)

        return store

    def store_wide(n, rows, y):
        wide[n, rows, :] = y

    gate(0, k_ref, v_ref)
    pl.semaphore_wait(barrier, blocks - 1 + n_tp - 1)
    start_all(0)
    gate(1, og_ref, q_ref)
    start_all(1)

    for part in range(4):
        load(4, part).wait()
    for n in range(blocks):
        wide[n] = filt_ref[:, n * TILE : (n + 1) * TILE].T
    outer_forward(lambda n, rows: wide[n, rows, :])
    get_fwd.wait()
    get_inv.wait()

    def each_bin(step):
        def group(i, carry):
            step([GROUP * i + g for g in range(GROUP)])
            return carry

        lax.fori_loop(0, bins // GROUP, group, 0)
        if bins % GROUP:
            step(list(range(bins - bins % GROUP, bins)))

    def filter_step(ks):
        specs = [apply(fwd, k, outer[k]) for k in ks]
        for k, spec in zip(ks, specs):
            spec_f[k] = spec

    each_bin(filter_step)

    arrive_all(0)
    outer_forward(lambda n, rows: recv[0, n, rows, :])

    def gated_step(ks):
        specs = [apply(fwd, k, outer[k]) for k in ks]
        products = [times(spec, spec_f[k], False) for k, spec in zip(ks, specs)]
        results = [apply(inv, k, product) for k, product in zip(ks, products)]
        for k, spec, result in zip(ks, specs, results):
            spec_kv[k] = spec
            back[k] = result

    each_bin(gated_step)
    outer_back(store_send(2))
    recv[2, me] = send[2, me]
    start_all(2)

    arrive_all(1)
    outer_forward(lambda n, rows: recv[1, n, rows, :])

    def gate_step(ks):
        specs = [apply(fwd, k, outer[k]) for k in ks]
        products = [times(spec, spec_f[k], True) for k, spec in zip(ks, specs)]
        results = [apply(inv, k, product) for k, product in zip(ks, products)]
        for k, spec, result in zip(ks, specs, results):
            spec_gg[k] = spec
            back[k] = result

    each_bin(gate_step)
    outer_back(store_send(3))
    recv[3, me] = send[3, me]
    start_all(3)

    def raw_step(ks):
        products = [times(spec_gg[k], spec_kv[k], True) for k in ks]
        results = [apply(inv, k, product) for k, product in zip(ks, products)]
        for k, result in zip(ks, results):
            back[k] = result

    each_bin(raw_step)
    outer_back(store_wide)
    total = jnp.zeros((8, TILE), F32)
    for n in range(blocks):
        tile = wide[n]
        raw_ref[:, n * TILE : (n + 1) * TILE] = tile.T
        total = total + jnp.sum((tile * tile).reshape(TILE // 8, 8, TILE), 0)
    put_raw = pltpu.make_async_copy(raw_ref, raw_hbm, raw_sem)
    put_raw.start()
    sq_mine[...] = total

    def tp_copy(j):
        return pltpu.make_async_remote_copy(
            src_ref=sq_mine,
            dst_ref=sq_tp.at[j - 1],
            send_sem=tp_send.at[j - 1],
            recv_sem=tp_recv.at[j - 1],
            device_id={"tp": lax.rem(my_tp + j, n_tp)},
            device_id_type=MESH,
        )

    for j in range(1, n_tp):
        tp_copy(j).start()
    for j in range(1, n_tp):
        tp_copy(j).wait()
        total = total + sq_tp[j - 1]
    sq_pair[...] = total
    sq_all[me] = total

    def sq_out(d):
        return pltpu.make_async_remote_copy(
            src_ref=sq_pair,
            dst_ref=sq_all.at[me],
            send_sem=sq_send.at[d],
            recv_sem=sq_recv.at[me],
            device_id=place(d),
            device_id_type=MESH,
        )

    def sq_in(s):
        return pltpu.make_async_remote_copy(
            src_ref=sq_pair,
            dst_ref=sq_all.at[s],
            send_sem=sq_send.at[s],
            recv_sem=sq_recv.at[s],
            device_id=place(s),
            device_id_type=MESH,
        )

    def sq_start(j, carry):
        sq_out(lax.rem(me + j, blocks)).start()
        return carry

    def sq_arrive(j, carry):
        sq_in(lax.rem(me + blocks - j, blocks)).wait_recv()
        return carry

    lax.fori_loop(1, blocks, sq_start, 0)

    def put(phase, hbm, s):
        return pltpu.make_async_copy(
            recv.at[phase, s],
            hbm.at[:, pl.ds(pl.multiple_of(s * TILE, TILE), TILE)],
            store_sem.at[phase - 2, s],
        )

    def put_all(phase, hbm):
        put(phase, hbm, me).start()

        def one(j, carry):
            s = lax.rem(me + blocks - j, blocks)
            in_copy(phase, s).wait_recv()
            put(phase, hbm, s).start()
            return carry

        lax.fori_loop(1, blocks, one, 0)

    put_all(2, co_hbm)
    lax.fori_loop(1, blocks, sq_arrive, 0)
    mean = jnp.sum(jnp.sum(sq_all[...], 0), keepdims=True) / entries
    rms = jnp.sqrt(mean + 1e-06)
    fac_ref[...] = jnp.minimum(1.0, 1.0 / rms)
    put_all(3, cg_hbm)

    def stored(s, carry):
        put(2, co_hbm, s).wait()
        put(3, cg_hbm, s).wait()
        return carry

    def sent(j, carry):
        d = lax.rem(me + j, blocks)
        for phase in range(4):
            out_copy(phase, d).wait_send()
        sq_out(d).wait_send()
        return carry

    lax.fori_loop(1, blocks, sent, 0)
    put_raw.wait()
    lax.fori_loop(0, blocks, stored, 0)


def finish_kernel(
    og_hbm, v_hbm, k_hbm, co_hbm, cg_hbm, raw_hbm, fac_ref,
    qg_hbm, kg_hbm, vg_hbm, fg_hbm,
    og, v, k, co, cg, raw, qg, kg, vg, fg, load_sem, store_sem,
):
    loads = ((og_hbm, og), (co_hbm, co), (cg_hbm, cg), (v_hbm, v), (k_hbm, k), (raw_hbm, raw))
    stores = ((qg, qg_hbm), (kg, kg_hbm), (vg, vg_hbm), (fg, fg_hbm))
    step = og.shape[0] // PARTS

    def copies(pairs, sems, part):
        rows = pl.ds(part * step, step)
        return [
            pltpu.make_async_copy(src.at[rows], dst.at[rows], sems.at[i, part])
            for i, (src, dst) in enumerate(pairs)
        ]

    for part in range(PARTS):
        for copy in copies(loads, load_sem, part):
            copy.start()
    for part in range(PARTS):
        for copy in copies(loads, load_sem, part):
            copy.wait()
        rows = slice(part * step, (part + 1) * step)
        qg[rows] = gated_product(og[rows], co[rows])
        grad = cg[rows]
        kg[rows] = gated_product(grad, v[rows])
        vg[rows] = gated_product(grad, k[rows])
        fg[rows] = raw[rows] * fac_ref[...]
        for copy in copies(stores, store_sem, part):
            copy.start()
    for part in range(PARTS):
        for copy in copies(stores, store_sem, part):
            copy.wait()


def fused_body(mesh, query_proj, key_proj, value_proj, output_grad, long_filter):
    n_blk, n_ctx, n_tp = mesh.shape["blk"], mesh.shape["ctx"], mesh.shape["tp"]
    blocks = n_blk * n_ctx
    bins = blocks + 1
    tokens, width = query_proj.shape
    chan_count, seq_length = long_filter.shape[1:]
    entries = float(chan_count * seq_length * blocks * n_tp)
    fwd, inv = inner_tables(blocks)
    vmem = pl.BlockSpec(memory_space=pltpu.VMEM)
    hbm = pl.BlockSpec(memory_space=pltpu.HBM)
    stream = pltpu.VMEM((tokens, width), BF16)
    lags = pltpu.VMEM((chan_count, seq_length), F32)
    dma = pltpu.SemaphoreType.DMA
    spec = pltpu.VMEM((bins, 2 * TILE, TILE), F32)
    flops = 6 * bins * 2 * 2 * TILE * 2 * TILE * TILE
    conv_out, conv_grad, filter_raw, factor = pl.pallas_call(
        functools.partial(fused_kernel, (blocks, n_ctx, n_tp, entries)),
        out_shape=(
            jax.ShapeDtypeStruct((tokens, width), BF16),
            jax.ShapeDtypeStruct((tokens, width), BF16),
            jax.ShapeDtypeStruct((chan_count, seq_length), F32),
            jax.ShapeDtypeStruct((1, 1), F32),
        ),
        in_specs=[hbm] * 7,
        out_specs=(hbm, hbm, hbm, vmem),
        scratch_shapes=[
            stream, stream, stream, stream, lags, lags,
            pltpu.VMEM(fwd.shape, BF16),
            pltpu.VMEM(inv.shape, BF16),
            pltpu.VMEM((4, blocks, TILE, TILE), BF16),
            pltpu.VMEM((4, blocks, TILE, TILE), BF16),
            pltpu.VMEM((bins, 2 * TILE, TILE), BF16),
            spec, spec, spec, spec,
            pltpu.VMEM((blocks, TILE, TILE), F32),
            pltpu.VMEM((8, TILE), F32),
            pltpu.VMEM((max(n_tp - 1, 1), 8, TILE), F32),
            pltpu.VMEM((8, TILE), F32),
            pltpu.VMEM((blocks, 8, TILE), F32),
            dma((5, 4)),
            dma((2, blocks)),
            dma(()),
            dma((2,)),
            dma((4, blocks)),
            dma((4, blocks)),
            dma((blocks,)),
            dma((blocks,)),
            dma((max(n_tp - 1, 1),)),
            dma((max(n_tp - 1, 1),)),
        ],
        compiler_params=pltpu.CompilerParams(
            collective_id=0, has_side_effects=True, vmem_limit_bytes=VMEM_LIMIT
        ),
        cost_estimate=pl.CostEstimate(
            flops=flops, bytes_accessed=16 * tokens * width, transcendentals=0
        ),
    )(
        key_proj, value_proj, query_proj, output_grad,
        long_filter.reshape(chan_count, seq_length),
        jnp.asarray(fwd), jnp.asarray(inv),
    )
    rows_like = jax.ShapeDtypeStruct((tokens, width), BF16)
    query_grad, key_grad, value_grad, filter_grad = pl.pallas_call(
        finish_kernel,
        out_shape=(rows_like,) * 3 + (jax.ShapeDtypeStruct((chan_count, seq_length), F32),),
        in_specs=[hbm] * 6 + [vmem],
        out_specs=(hbm,) * 4,
        scratch_shapes=[stream] * 5 + [lags] + [stream] * 3 + [lags, dma((6, PARTS)), dma((4, PARTS))],
        compiler_params=pltpu.CompilerParams(vmem_limit_bytes=VMEM_LIMIT),
        cost_estimate=pl.CostEstimate(
            flops=4 * tokens * width, bytes_accessed=24 * tokens * width, transcendentals=0
        ),
    )(output_grad, value_proj, key_proj, conv_out, conv_grad, filter_raw, factor)
    filter_grad = filter_grad.reshape(1, chan_count, seq_length)
    return (query_grad, key_grad, value_grad, filter_grad)


def general_body(query_proj, key_proj, value_proj, output_grad, long_filter):
    axes = ("blk", "ctx")
    chan_count = long_filter.shape[1]
    seq_length = long_filter.shape[2]
    kernel_cols = long_filter.reshape(chan_count, seq_length)

    def to_channels(rows):
        return lax.all_to_all(rows.T, axes, split_axis=0, concat_axis=1, tiled=True)

    def to_tokens(cols):
        return lax.all_to_all(cols, axes, split_axis=1, concat_axis=0, tiled=True).T

    gated_cols = to_channels(gated_product(key_proj, value_proj))
    gate_cols = to_channels(gated_product(output_grad, query_proj))
    conv_out, conv_grad, filter_raw = channel_work(gated_cols, gate_cols, kernel_cols)
    conv_out, conv_grad = to_tokens(conv_out), to_tokens(conv_grad)
    query_grad = gated_product(output_grad, conv_out)
    key_grad = gated_product(conv_grad, value_proj)
    value_grad = gated_product(conv_grad, key_proj)
    square_total = lax.psum(jnp.sum(filter_raw * filter_raw), ("blk", "ctx", "tp"))
    entry_count = (
        chan_count * seq_length * lax.axis_size("blk") * lax.axis_size("ctx") * lax.axis_size("tp")
    )
    grad_rms = jnp.sqrt(square_total / entry_count + 1e-06)
    factor = jnp.minimum(1.0, 1.0 / grad_rms)
    filter_grad = (filter_raw * factor).reshape(1, chan_count, seq_length)
    return (query_grad, key_grad, value_grad, filter_grad)


def body(mesh, *args):
    blocks = mesh.shape["blk"] * mesh.shape["ctx"]
    fits = args[0].shape[0] == TILE and args[4].shape[1] == TILE and blocks in (4, 8, 16)
    if fits:
        return fused_body(mesh, *args)
    return general_body(*args)


def solution(mesh):
    in_specs = (
        P(("blk", "ctx"), "tp"),
        P(("blk", "ctx"), "tp"),
        P(("blk", "ctx"), "tp"),
        P(("blk", "ctx"), "tp"),
        P("tp", ("blk", "ctx"), None),
    )
    out_specs = (
        P(("blk", "ctx"), "tp"),
        P(("blk", "ctx"), "tp"),
        P(("blk", "ctx"), "tp"),
        P("tp", ("blk", "ctx"), None),
    )
    return jax.shard_map(
        functools.partial(body, mesh), mesh=mesh, in_specs=in_specs, out_specs=out_specs, check_vma=False
    )
```

```python
import functools
import math

import jax
import jax.numpy as jnp
import ml_dtypes
import numpy as np
from jax import lax
from jax.experimental import pallas as pl
from jax.experimental.pallas import tpu as pltpu
from jax.sharding import PartitionSpec as P

PRECISE = lax.Precision.HIGH
MESH = pl.DeviceIdType.MESH
TILE = 128
PARTS = 4
CHUNK = 16
GROUP = 4
VMEM_LIMIT = 63 * 1024 * 1024
F32 = jnp.float32
BF16 = jnp.bfloat16


def spectrum_tables(seq_length):
    outer_size = seq_length // 64
    half_size = outer_size // 2
    full_size = outer_size * 128
    row_index = lax.broadcasted_iota(jnp.int32, (outer_size, half_size), 0)
    col_index = lax.broadcasted_iota(jnp.int32, (outer_size, half_size), 1)
    outer_angle = (row_index * col_index % outer_size).astype(jnp.float32) * (
        2.0 * math.pi / outer_size
    )
    inner_row = lax.broadcasted_iota(jnp.int32, (128, 128), 0)
    inner_col = lax.broadcasted_iota(jnp.int32, (128, 128), 1)
    inner_angle = (inner_row * inner_col % 128).astype(jnp.float32) * (2.0 * math.pi / 128)
    twist_row = lax.broadcasted_iota(jnp.int32, (outer_size, 128), 0)
    twist_col = lax.broadcasted_iota(jnp.int32, (outer_size, 128), 1)
    twist_angle = (twist_row * twist_col % full_size).astype(jnp.float32) * (
        2.0 * math.pi / full_size
    )
    return (
        jnp.cos(outer_angle),
        jnp.sin(outer_angle),
        jnp.cos(inner_angle),
        jnp.sin(inner_angle),
        jnp.cos(twist_angle),
        jnp.sin(twist_angle),
        full_size,
    )


def to_spectrum(signal, tables):
    outer_cos, outer_sin, inner_cos, inner_sin, twist_cos, twist_sin, full_size = tables
    blocks = signal.reshape(signal.shape[0], outer_cos.shape[1], 128)
    first_real = jnp.einsum("kn,cnm->ckm", outer_cos, blocks, precision=PRECISE)
    first_imag = -jnp.einsum("kn,cnm->ckm", outer_sin, blocks, precision=PRECISE)
    turned_real = first_real * twist_cos + first_imag * twist_sin
    turned_imag = first_imag * twist_cos - first_real * twist_sin
    real_part = jnp.einsum("ckm,mj->ckj", turned_real, inner_cos, precision=PRECISE) + jnp.einsum(
        "ckm,mj->ckj", turned_imag, inner_sin, precision=PRECISE
    )
    imag_part = jnp.einsum("ckm,mj->ckj", turned_imag, inner_cos, precision=PRECISE) - jnp.einsum(
        "ckm,mj->ckj", turned_real, inner_sin, precision=PRECISE
    )
    return (real_part, imag_part)


def from_spectrum(spectrum, tables):
    outer_cos, outer_sin, inner_cos, inner_sin, twist_cos, twist_sin, full_size = tables
    real_part, imag_part = spectrum
    mixed_real = jnp.einsum("ckm,mj->ckj", real_part, inner_cos, precision=PRECISE) - jnp.einsum(
        "ckm,mj->ckj", imag_part, inner_sin, precision=PRECISE
    )
    mixed_imag = jnp.einsum("ckm,mj->ckj", imag_part, inner_cos, precision=PRECISE) + jnp.einsum(
        "ckm,mj->ckj", real_part, inner_sin, precision=PRECISE
    )
    turned_real = mixed_real * twist_cos - mixed_imag * twist_sin
    turned_imag = mixed_imag * twist_cos + mixed_real * twist_sin
    signal = jnp.einsum("kn,ckm->cnm", outer_cos, turned_real, precision=PRECISE) - jnp.einsum(
        "kn,ckm->cnm", outer_sin, turned_imag, precision=PRECISE
    )
    return (signal / full_size).reshape(signal.shape[0], -1)


def complex_product(left, right, conjugate):
    left_real, left_imag = left
    right_real, right_imag = right
    if conjugate:
        return (
            left_real * right_real + left_imag * right_imag,
            left_imag * right_real - left_real * right_imag,
        )
    return (
        left_real * right_real - left_imag * right_imag,
        left_real * right_imag + left_imag * right_real,
    )


def channel_work(gated_cols, gate_cols, kernel_cols):
    tables = spectrum_tables(kernel_cols.shape[1])
    kernel_spec = to_spectrum(kernel_cols, tables)
    gated_spec = to_spectrum(gated_cols.astype(jnp.float32), tables)
    gate_spec = to_spectrum(gate_cols.astype(jnp.float32), tables)
    conv_out = from_spectrum(complex_product(gated_spec, kernel_spec, False), tables).astype(
        jnp.bfloat16
    )
    conv_grad = from_spectrum(complex_product(gate_spec, kernel_spec, True), tables).astype(
        jnp.bfloat16
    )
    filter_raw = from_spectrum(complex_product(gate_spec, gated_spec, True), tables)
    return (conv_out, conv_grad, filter_raw)


def gated_product(left, right):
    return (left.astype(jnp.float32) * right.astype(jnp.float32)).astype(jnp.bfloat16)


def turn(value, step, span):
    re, im = value
    step = step % span
    if step == 0:
        return value
    if 4 * step == span:
        return (im, -re)
    if 2 * step == span:
        return (-re, -im)
    if 4 * step == 3 * span:
        return (-im, re)
    c = math.cos(2.0 * math.pi * step / span)
    s = math.sin(2.0 * math.pi * step / span)
    if (8 * step) % span == 0:
        r = abs(c)
        a, b = r * (re + im), r * (im - re)
        eighth = 8 * step // span
        return {1: (a, b), 3: (b, -a), 5: (-a, -b), 7: (-b, a)}[eighth]
    return (c * re + s * im, c * im - s * re)


def complex_dft(values, way):
    n = len(values)
    if n == 1:
        return values
    even = complex_dft(values[0::2], way)
    odd = complex_dft(values[1::2], way)
    out = [None] * n
    for k in range(n // 2):
        tr, ti = turn(odd[k], way * k, n)
        er, ei = even[k]
        out[k] = (er + tr, ei + ti)
        out[k + n // 2] = (er - tr, ei - ti)
    return out


def odd_bins(d, span):
    q = span // 4
    z = [turn((d[n], -d[n + q]), n, span) for n in range(q)]
    out = {}
    for m, (re, im) in enumerate(complex_dft(z, 1)):
        k = 4 * m + 1
        if k < span // 2:
            out[k] = (re, im)
        else:
            out[span - k] = (re, -im)
    return out


def real_bins(x):
    n = len(x)
    if n == 1:
        return {0: (x[0], None)}
    h = n // 2
    out = {2 * k: v for k, v in real_bins([x[i] + x[i + h] for i in range(h)]).items()}
    d = [x[i] - x[i + h] for i in range(h)]
    if n == 2:
        out[1] = (d[0], None)
    else:
        out.update(odd_bins(d, n))
    return out


def padded_bins(x):
    out = {2 * k: v for k, v in real_bins(x).items()}
    out.update(odd_bins(x, 2 * len(x)))
    return out


def odd_back(bins, span):
    q = span // 4
    c = []
    for m in range(q):
        k = 4 * m + 1
        if k < span // 2:
            c.append(bins[k])
        else:
            re, im = bins[span - k]
            c.append((re, -im))
    w = [turn(v, -n, span) for n, v in enumerate(complex_dft(c, -1))]
    return [v[0] for v in w] + [-v[1] for v in w]


def real_back(bins, n):
    if n == 1:
        return [bins[0][0]]
    if n == 2:
        return [bins[0][0] + bins[1][0], bins[0][0] - bins[1][0]]
    h = n // 2
    e = real_back({k // 2: bins[k] for k in bins if k % 2 == 0}, h)
    o = odd_back({k: bins[k] for k in bins if k % 2 == 1}, n)
    return [a + b for a, b in zip(e, o)] + [a - b for a, b in zip(e, o)]


def padded_back(bins, n):
    e = real_back({k // 2: bins[k] for k in bins if k % 2 == 0}, n)
    o = odd_back({k: bins[k] for k in bins if k % 2 == 1}, 2 * n)
    return [a + b for a, b in zip(e, o)]


def inner_tables(blocks):
    span = 2 * blocks
    full = span * TILE
    k1 = np.arange(blocks + 1).reshape(-1, 1, 1)
    k2 = np.arange(TILE).reshape(1, -1, 1)
    n2 = np.arange(TILE).reshape(1, 1, -1)
    angle = (n2 * (k1 + span * k2) % full) * (2.0 * math.pi / full)
    c, s = np.cos(angle), np.sin(angle)
    fwd = np.concatenate(
        [np.concatenate([c, s], 2), np.concatenate([-s, c], 2)], 1
    )
    weight = np.where((k1 == 0) | (k1 == blocks), 1.0, 2.0) / full
    inv = fwd.transpose(0, 2, 1) * weight

    return fwd.astype(ml_dtypes.bfloat16), inv.astype(ml_dtypes.bfloat16)


def fused_kernel(
    cfg,
    k_hbm, v_hbm, q_hbm, og_hbm, filt_hbm, fwd_hbm, inv_hbm,
    qg_hbm, kg_hbm, vg_hbm, raw_hbm, fac_ref,
    k_ref, v_ref, q_ref, og_ref, filt_ref, raw_ref, fwd, inv, send, recv, outer, spec_f, spec_kv, spec_gg, back, wide,
    sq_mine, sq_tp, sq_pair, sq_all,
    load_sem, store_sem, raw_sem, table_sem, send_sem, recv_sem, sq_send, sq_recv, tp_send, tp_recv,
):
    blocks, n_ctx, n_tp, entries = cfg
    me = lax.axis_index("blk") * n_ctx + lax.axis_index("ctx")
    my_tp = lax.axis_index("tp")
    bins = blocks + 1

    def place(d):
        return {"blk": d // n_ctx, "ctx": d % n_ctx}

    quarter = k_ref.shape[1] // 4

    def load(which, part):
        hbm, vmem = (
            (k_hbm, k_ref), (v_hbm, v_ref), (og_hbm, og_ref), (q_hbm, q_ref), (filt_hbm, filt_ref)
        )[which]
        cols = pl.ds(part * quarter, quarter)
        return pltpu.make_async_copy(
            hbm.at[:, cols], vmem.at[:, cols], load_sem.at[which, part]
        )

    for pair in ((0, 1), (2, 3), (4,)):
        for part in range(4):
            for which in pair:
                load(which, part).start()
    get_fwd = pltpu.make_async_copy(fwd_hbm, fwd, table_sem.at[0])
    get_inv = pltpu.make_async_copy(inv_hbm, inv, table_sem.at[1])
    get_fwd.start()
    get_inv.start()

    barrier = pltpu.get_barrier_semaphore()

    def greet(j, carry):
        d = lax.rem(me + j, blocks)
        pl.semaphore_signal(barrier, inc=1, device_id=place(d), device_id_type=MESH)
        return carry

    lax.fori_loop(1, blocks, greet, 0)
    for j in range(1, n_tp):
        pl.semaphore_signal(
            barrier, inc=1, device_id={"tp": lax.rem(my_tp + j, n_tp)}, device_id_type=MESH
        )

    def gate(phase, a_ref, b_ref):
        for d in range(blocks):
            if d % (blocks // 4) == 0:
                load(2 * phase, d // (blocks // 4)).wait()
                load(2 * phase + 1, d // (blocks // 4)).wait()
            cols = slice(d * TILE, (d + 1) * TILE)
            send[phase, d] = gated_product(a_ref[:, cols], b_ref[:, cols])
        recv[phase, me] = send[phase, me]

    def out_copy(phase, d):
        return pltpu.make_async_remote_copy(
            src_ref=send.at[phase, d],
            dst_ref=recv.at[phase, me],
            send_sem=send_sem.at[phase, d],
            recv_sem=recv_sem.at[phase, me],
            device_id=place(d),
            device_id_type=MESH,
        )

    def in_copy(phase, s):
        return pltpu.make_async_remote_copy(
            src_ref=send.at[phase, s],
            dst_ref=recv.at[phase, s],
            send_sem=send_sem.at[phase, s],
            recv_sem=recv_sem.at[phase, s],
            device_id=place(s),
            device_id_type=MESH,
        )

    def flipped(place_on_axis, mask):
        out, weight = 0, 1
        while weight < n_ctx:
            bit = lax.rem(place_on_axis // weight, 2)
            out = out + weight * (1 - bit if mask & weight else bit)
            weight *= 2
        return out

    def start_all(phase, after=None):
        for mask in range(n_ctx - 1, -1, -1):
            ctx = flipped(lax.axis_index("ctx"), mask)

            def one(j, carry, ctx=ctx):
                blk = lax.rem(lax.axis_index("blk") + j, blocks // n_ctx)
                if after is not None:
                    out_copy(after, blk * n_ctx + ctx).wait_send()
                out_copy(phase, blk * n_ctx + ctx).start()
                return carry

            lax.fori_loop(0 if mask else 1, blocks // n_ctx, one, 0)

    def arrive_all(phase):
        def one(j, carry):
            in_copy(phase, lax.rem(me + blocks - j, blocks)).wait_recv()
            return carry

        lax.fori_loop(1, blocks, one, 0)

    def rows_at(i):
        return pl.ds(pl.multiple_of(i * CHUNK, CHUNK), CHUNK)

    def outer_forward(load):
        def one(i, carry):
            rows = rows_at(i)
            out = padded_bins([load(n, rows).astype(F32) for n in range(blocks)])
            low = pl.ds(pl.multiple_of(TILE + i * CHUNK, CHUNK), CHUNK)
            for k in range(bins):
                re, im = out[k]
                outer[k, rows, :] = re.astype(BF16)
                outer[k, low, :] = (jnp.zeros_like(re) if im is None else im).astype(BF16)
            return carry

        lax.fori_loop(0, TILE // CHUNK, one, 0)

    def apply(table, k, value):
        return jnp.dot(table[k], value, preferred_element_type=F32)

    def times(a, b, conjugate):
        ar, ai = a[:TILE], a[TILE:]
        br, bi = b[:TILE], b[TILE:]
        if conjugate:
            return jnp.concatenate([ar * br + ai * bi, ai * br - ar * bi], 0).astype(BF16)
        return jnp.concatenate([ar * br - ai * bi, ar * bi + ai * br], 0).astype(BF16)

    def outer_back(store):
        def one(i, carry):
            rows = rows_at(i)
            low = pl.ds(pl.multiple_of(TILE + i * CHUNK, CHUNK), CHUNK)
            got = {k: (back[k, rows, :], back[k, low, :]) for k in range(bins)}
            for n, y in enumerate(padded_back(got, blocks)):
                store(n, rows, y)
            return carry

        lax.fori_loop(0, TILE // CHUNK, one, 0)

    def store_send(phase):
        def store(n, rows, y):
            send[phase, n, rows, :] = y.astype(BF16)

        return store

    def store_wide(n, rows, y):
        wide[n, rows, :] = y

    gate(0, k_ref, v_ref)
    pl.semaphore_wait(barrier, blocks - 1 + n_tp - 1)
    start_all(0)
    gate(1, og_ref, q_ref)

    for part in range(4):
        load(4, part).wait()
    for n in range(blocks):
        wide[n] = filt_ref[:, n * TILE : (n + 1) * TILE].T
    outer_forward(lambda n, rows: wide[n, rows, :])
    get_fwd.wait()
    get_inv.wait()

    def each_bin(step):
        def group(i, carry):
            step([GROUP * i + g for g in range(GROUP)])
            return carry

        lax.fori_loop(0, bins // GROUP, group, 0)
        if bins % GROUP:
            step(list(range(bins - bins % GROUP, bins)))

    def filter_step(ks):
        specs = [apply(fwd, k, outer[k]) for k in ks]
        for k, spec in zip(ks, specs):
            spec_f[k] = spec

    each_bin(filter_step)
    start_all(1, after=0)

    arrive_all(0)
    outer_forward(lambda n, rows: recv[0, n, rows, :])

    def gated_step(ks):
        specs = [apply(fwd, k, outer[k]) for k in ks]
        products = [times(spec, spec_f[k], False) for k, spec in zip(ks, specs)]
        results = [apply(inv, k, product) for k, product in zip(ks, products)]
        for k, spec, result in zip(ks, specs, results):
            spec_kv[k] = spec
            back[k] = result

    each_bin(gated_step)
    outer_back(store_send(2))
    recv[2, me] = send[2, me]
    start_all(2)

    arrive_all(1)
    outer_forward(lambda n, rows: recv[1, n, rows, :])

    def gate_step(ks):
        specs = [apply(fwd, k, outer[k]) for k in ks]
        products = [times(spec, spec_f[k], True) for k, spec in zip(ks, specs)]
        results = [apply(inv, k, product) for k, product in zip(ks, products)]
        for k, spec, result in zip(ks, specs, results):
            spec_gg[k] = spec
            back[k] = result

    each_bin(gate_step)
    outer_back(store_send(3))
    recv[3, me] = send[3, me]
    start_all(3)

    def raw_step(ks):
        products = [times(spec_gg[k], spec_kv[k], True) for k in ks]
        results = [apply(inv, k, product) for k, product in zip(ks, products)]
        for k, result in zip(ks, results):
            back[k] = result

    each_bin(raw_step)
    outer_back(store_wide)
    total = jnp.zeros((8, TILE), F32)
    for n in range(blocks):
        tile = wide[n]
        raw_ref[:, n * TILE : (n + 1) * TILE] = tile.T
        total = total + jnp.sum((tile * tile).reshape(TILE // 8, 8, TILE), 0)
    put_raw = pltpu.make_async_copy(raw_ref, raw_hbm, raw_sem)
    put_raw.start()
    sq_mine[...] = total

    def tp_copy(j):
        return pltpu.make_async_remote_copy(
            src_ref=sq_mine,
            dst_ref=sq_tp.at[j - 1],
            send_sem=tp_send.at[j - 1],
            recv_sem=tp_recv.at[j - 1],
            device_id={"tp": lax.rem(my_tp + j, n_tp)},
            device_id_type=MESH,
        )

    for j in range(1, n_tp):
        tp_copy(j).start()
    for j in range(1, n_tp):
        tp_copy(j).wait()
        total = total + sq_tp[j - 1]
    sq_pair[...] = total
    sq_all[me] = total

    def sq_out(d):
        return pltpu.make_async_remote_copy(
            src_ref=sq_pair,
            dst_ref=sq_all.at[me],
            send_sem=sq_send.at[d],
            recv_sem=sq_recv.at[me],
            device_id=place(d),
            device_id_type=MESH,
        )

    def sq_in(s):
        return pltpu.make_async_remote_copy(
            src_ref=sq_pair,
            dst_ref=sq_all.at[s],
            send_sem=sq_send.at[s],
            recv_sem=sq_recv.at[s],
            device_id=place(s),
            device_id_type=MESH,
        )

    def sq_start(j, carry):
        sq_out(lax.rem(me + j, blocks)).start()
        return carry

    def sq_arrive(j, carry):
        sq_in(lax.rem(me + blocks - j, blocks)).wait_recv()
        return carry

    lax.fori_loop(1, blocks, sq_start, 0)

    def columns(s):
        return pl.ds(pl.multiple_of(s * TILE, TILE), TILE)

    def put(which, s):
        hbm, slot = ((qg_hbm, 2), (kg_hbm, 3), (vg_hbm, 0))[which]
        return pltpu.make_async_copy(
            recv.at[slot, s], hbm.at[:, columns(s)], store_sem.at[which, s]
        )

    def finish_query(s):
        recv[2, s] = gated_product(og_ref[:, columns(s)], recv[2, s])
        put(0, s).start()

    def finish_grad(s):
        grad = recv[3, s]
        recv[3, s] = gated_product(grad, v_ref[:, columns(s)])
        put(1, s).start()
        recv[0, s] = gated_product(grad, k_ref[:, columns(s)])
        put(2, s).start()

    def finish_all(phase, finish):
        finish(me)

        def one(j, carry):
            s = lax.rem(me + blocks - j, blocks)
            in_copy(phase, s).wait_recv()
            finish(s)
            return carry

        lax.fori_loop(1, blocks, one, 0)

    finish_all(2, finish_query)
    lax.fori_loop(1, blocks, sq_arrive, 0)
    mean = jnp.sum(jnp.sum(sq_all[...], 0), keepdims=True) / entries
    rms = jnp.sqrt(mean + 1e-06)
    fac_ref[...] = jnp.minimum(1.0, 1.0 / rms)
    finish_all(3, finish_grad)

    def stored(s, carry):
        for which in range(3):
            put(which, s).wait()
        return carry

    def sent(j, carry):
        d = lax.rem(me + j, blocks)
        for phase in range(1, 4):
            out_copy(phase, d).wait_send()
        sq_out(d).wait_send()
        return carry

    lax.fori_loop(1, blocks, sent, 0)
    put_raw.wait()
    lax.fori_loop(0, blocks, stored, 0)


def finish_kernel(
    qg_in, kg_in, vg_in, raw_hbm, fac_ref, qg_out, kg_out, vg_out, fg_hbm,
    raw, fg, move_sem, load_sem, store_sem,
):
    step = raw.shape[0] // PARTS

    def copy(src, dst, sem, part):
        rows = pl.ds(part * step, step)
        return pltpu.make_async_copy(src.at[rows], dst.at[rows], sem)

    loads = [copy(raw_hbm, raw, load_sem.at[p], p) for p in range(PARTS)]
    stores = [copy(fg, fg_hbm, store_sem.at[p], p) for p in range(PARTS)]
    moves = [
        copy(src, dst, move_sem.at[i, p], p)
        for p in range(PARTS)
        for i, (src, dst) in enumerate(((qg_in, qg_out), (kg_in, kg_out), (vg_in, vg_out)))
    ]
    for item in loads + moves:
        item.start()
    for p in range(PARTS):
        loads[p].wait()
        rows = slice(p * step, (p + 1) * step)
        fg[rows] = raw[rows] * fac_ref[...]
        stores[p].start()
    for item in moves + stores:
        item.wait()


def fused_body(mesh, query_proj, key_proj, value_proj, output_grad, long_filter):
    n_blk, n_ctx, n_tp = mesh.shape["blk"], mesh.shape["ctx"], mesh.shape["tp"]
    blocks = n_blk * n_ctx
    bins = blocks + 1
    tokens, width = query_proj.shape
    chan_count, seq_length = long_filter.shape[1:]
    entries = float(chan_count * seq_length * blocks * n_tp)
    fwd, inv = inner_tables(blocks)
    vmem = pl.BlockSpec(memory_space=pltpu.VMEM)
    hbm = pl.BlockSpec(memory_space=pltpu.HBM)
    stream = pltpu.VMEM((tokens, width), BF16)
    lags = pltpu.VMEM((chan_count, seq_length), F32)
    dma = pltpu.SemaphoreType.DMA
    spec = pltpu.VMEM((bins, 2 * TILE, TILE), F32)
    rows_like = jax.ShapeDtypeStruct((tokens, width), BF16)
    flops = 6 * bins * 2 * 2 * TILE * 2 * TILE * TILE
    query_part, key_part, value_part, filter_raw, factor = pl.pallas_call(
        functools.partial(fused_kernel, (blocks, n_ctx, n_tp, entries)),
        out_shape=(
            rows_like, rows_like, rows_like,
            jax.ShapeDtypeStruct((chan_count, seq_length), F32),
            jax.ShapeDtypeStruct((1, 1), F32),
        ),
        in_specs=[hbm] * 7,
        out_specs=(hbm, hbm, hbm, hbm, vmem),
        scratch_shapes=[
            stream, stream, stream, stream, lags, lags,
            pltpu.VMEM(fwd.shape, BF16),
            pltpu.VMEM(inv.shape, BF16),
            pltpu.VMEM((4, blocks, TILE, TILE), BF16),
            pltpu.VMEM((4, blocks, TILE, TILE), BF16),
            pltpu.VMEM((bins, 2 * TILE, TILE), BF16),
            spec, spec, spec, spec,
            pltpu.VMEM((blocks, TILE, TILE), F32),
            pltpu.VMEM((8, TILE), F32),
            pltpu.VMEM((max(n_tp - 1, 1), 8, TILE), F32),
            pltpu.VMEM((8, TILE), F32),
            pltpu.VMEM((blocks, 8, TILE), F32),
            dma((5, 4)),
            dma((3, blocks)),
            dma(()),
            dma((2,)),
            dma((4, blocks)),
            dma((4, blocks)),
            dma((blocks,)),
            dma((blocks,)),
            dma((max(n_tp - 1, 1),)),
            dma((max(n_tp - 1, 1),)),
        ],
        compiler_params=pltpu.CompilerParams(
            collective_id=0, has_side_effects=True, vmem_limit_bytes=VMEM_LIMIT
        ),
        cost_estimate=pl.CostEstimate(
            flops=flops, bytes_accessed=16 * tokens * width, transcendentals=0
        ),
    )(
        key_proj, value_proj, query_proj, output_grad,
        long_filter.reshape(chan_count, seq_length),
        jnp.asarray(fwd), jnp.asarray(inv),
    )
    query_grad, key_grad, value_grad, filter_grad = pl.pallas_call(
        finish_kernel,
        out_shape=(rows_like,) * 3 + (jax.ShapeDtypeStruct((chan_count, seq_length), F32),),
        in_specs=[hbm] * 4 + [vmem],
        out_specs=(hbm,) * 4,
        scratch_shapes=[lags, lags, dma((3, PARTS)), dma((PARTS,)), dma((PARTS,))],
        compiler_params=pltpu.CompilerParams(vmem_limit_bytes=VMEM_LIMIT),
        cost_estimate=pl.CostEstimate(
            flops=tokens * width, bytes_accessed=20 * tokens * width, transcendentals=0
        ),
    )(query_part, key_part, value_part, filter_raw, factor)
    filter_grad = filter_grad.reshape(1, chan_count, seq_length)
    return (query_grad, key_grad, value_grad, filter_grad)


def general_body(query_proj, key_proj, value_proj, output_grad, long_filter):
    axes = ("blk", "ctx")
    chan_count = long_filter.shape[1]
    seq_length = long_filter.shape[2]
    kernel_cols = long_filter.reshape(chan_count, seq_length)

    def to_channels(rows):
        return lax.all_to_all(rows.T, axes, split_axis=0, concat_axis=1, tiled=True)

    def to_tokens(cols):
        return lax.all_to_all(cols, axes, split_axis=1, concat_axis=0, tiled=True).T

    gated_cols = to_channels(gated_product(key_proj, value_proj))
    gate_cols = to_channels(gated_product(output_grad, query_proj))
    conv_out, conv_grad, filter_raw = channel_work(gated_cols, gate_cols, kernel_cols)
    conv_out, conv_grad = to_tokens(conv_out), to_tokens(conv_grad)
    query_grad = gated_product(output_grad, conv_out)
    key_grad = gated_product(conv_grad, value_proj)
    value_grad = gated_product(conv_grad, key_proj)
    square_total = lax.psum(jnp.sum(filter_raw * filter_raw), ("blk", "ctx", "tp"))
    entry_count = (
        chan_count * seq_length * lax.axis_size("blk") * lax.axis_size("ctx") * lax.axis_size("tp")
    )
    grad_rms = jnp.sqrt(square_total / entry_count + 1e-06)
    factor = jnp.minimum(1.0, 1.0 / grad_rms)
    filter_grad = (filter_raw * factor).reshape(1, chan_count, seq_length)
    return (query_grad, key_grad, value_grad, filter_grad)


def body(mesh, *args):
    blocks = mesh.shape["blk"] * mesh.shape["ctx"]
    fits = args[0].shape[0] == TILE and args[4].shape[1] == TILE and blocks in (4, 8, 16)
    if fits:
        return fused_body(mesh, *args)
    return general_body(*args)


def solution(mesh):
    in_specs = (
        P(("blk", "ctx"), "tp"),
        P(("blk", "ctx"), "tp"),
        P(("blk", "ctx"), "tp"),
        P(("blk", "ctx"), "tp"),
        P("tp", ("blk", "ctx"), None),
    )
    out_specs = (
        P(("blk", "ctx"), "tp"),
        P(("blk", "ctx"), "tp"),
        P(("blk", "ctx"), "tp"),
        P("tp", ("blk", "ctx"), None),
    )
    return jax.shard_map(
        functools.partial(body, mesh), mesh=mesh, in_specs=in_specs, out_specs=out_specs, check_vma=False
    )
```

```python
import functools
import math

import jax
import jax.numpy as jnp
import ml_dtypes
import numpy as np
from jax import lax
from jax.experimental import pallas as pl
from jax.experimental.pallas import tpu as pltpu
from jax.sharding import PartitionSpec as P

PRECISE = lax.Precision.HIGH
MESH = pl.DeviceIdType.MESH
TILE = 128
PARTS = 4
CHUNK = 16
GROUP = 4
VMEM_LIMIT = 63 * 1024 * 1024
F32 = jnp.float32
BF16 = jnp.bfloat16


def spectrum_tables(seq_length):
    outer_size = seq_length // 64
    half_size = outer_size // 2
    full_size = outer_size * 128
    row_index = lax.broadcasted_iota(jnp.int32, (outer_size, half_size), 0)
    col_index = lax.broadcasted_iota(jnp.int32, (outer_size, half_size), 1)
    outer_angle = (row_index * col_index % outer_size).astype(jnp.float32) * (
        2.0 * math.pi / outer_size
    )
    inner_row = lax.broadcasted_iota(jnp.int32, (128, 128), 0)
    inner_col = lax.broadcasted_iota(jnp.int32, (128, 128), 1)
    inner_angle = (inner_row * inner_col % 128).astype(jnp.float32) * (2.0 * math.pi / 128)
    twist_row = lax.broadcasted_iota(jnp.int32, (outer_size, 128), 0)
    twist_col = lax.broadcasted_iota(jnp.int32, (outer_size, 128), 1)
    twist_angle = (twist_row * twist_col % full_size).astype(jnp.float32) * (
        2.0 * math.pi / full_size
    )
    return (
        jnp.cos(outer_angle),
        jnp.sin(outer_angle),
        jnp.cos(inner_angle),
        jnp.sin(inner_angle),
        jnp.cos(twist_angle),
        jnp.sin(twist_angle),
        full_size,
    )


def to_spectrum(signal, tables):
    outer_cos, outer_sin, inner_cos, inner_sin, twist_cos, twist_sin, full_size = tables
    blocks = signal.reshape(signal.shape[0], outer_cos.shape[1], 128)
    first_real = jnp.einsum("kn,cnm->ckm", outer_cos, blocks, precision=PRECISE)
    first_imag = -jnp.einsum("kn,cnm->ckm", outer_sin, blocks, precision=PRECISE)
    turned_real = first_real * twist_cos + first_imag * twist_sin
    turned_imag = first_imag * twist_cos - first_real * twist_sin
    real_part = jnp.einsum("ckm,mj->ckj", turned_real, inner_cos, precision=PRECISE) + jnp.einsum(
        "ckm,mj->ckj", turned_imag, inner_sin, precision=PRECISE
    )
    imag_part = jnp.einsum("ckm,mj->ckj", turned_imag, inner_cos, precision=PRECISE) - jnp.einsum(
        "ckm,mj->ckj", turned_real, inner_sin, precision=PRECISE
    )
    return (real_part, imag_part)


def from_spectrum(spectrum, tables):
    outer_cos, outer_sin, inner_cos, inner_sin, twist_cos, twist_sin, full_size = tables
    real_part, imag_part = spectrum
    mixed_real = jnp.einsum("ckm,mj->ckj", real_part, inner_cos, precision=PRECISE) - jnp.einsum(
        "ckm,mj->ckj", imag_part, inner_sin, precision=PRECISE
    )
    mixed_imag = jnp.einsum("ckm,mj->ckj", imag_part, inner_cos, precision=PRECISE) + jnp.einsum(
        "ckm,mj->ckj", real_part, inner_sin, precision=PRECISE
    )
    turned_real = mixed_real * twist_cos - mixed_imag * twist_sin
    turned_imag = mixed_imag * twist_cos + mixed_real * twist_sin
    signal = jnp.einsum("kn,ckm->cnm", outer_cos, turned_real, precision=PRECISE) - jnp.einsum(
        "kn,ckm->cnm", outer_sin, turned_imag, precision=PRECISE
    )
    return (signal / full_size).reshape(signal.shape[0], -1)


def complex_product(left, right, conjugate):
    left_real, left_imag = left
    right_real, right_imag = right
    if conjugate:
        return (
            left_real * right_real + left_imag * right_imag,
            left_imag * right_real - left_real * right_imag,
        )
    return (
        left_real * right_real - left_imag * right_imag,
        left_real * right_imag + left_imag * right_real,
    )


def channel_work(gated_cols, gate_cols, kernel_cols):
    tables = spectrum_tables(kernel_cols.shape[1])
    kernel_spec = to_spectrum(kernel_cols, tables)
    gated_spec = to_spectrum(gated_cols.astype(jnp.float32), tables)
    gate_spec = to_spectrum(gate_cols.astype(jnp.float32), tables)
    conv_out = from_spectrum(complex_product(gated_spec, kernel_spec, False), tables).astype(
        jnp.bfloat16
    )
    conv_grad = from_spectrum(complex_product(gate_spec, kernel_spec, True), tables).astype(
        jnp.bfloat16
    )
    filter_raw = from_spectrum(complex_product(gate_spec, gated_spec, True), tables)
    return (conv_out, conv_grad, filter_raw)


def gated_product(left, right):
    return (left.astype(jnp.float32) * right.astype(jnp.float32)).astype(jnp.bfloat16)


def turn(value, step, span):
    re, im = value
    step = step % span
    if step == 0:
        return value
    if 4 * step == span:
        return (im, -re)
    if 2 * step == span:
        return (-re, -im)
    if 4 * step == 3 * span:
        return (-im, re)
    c = math.cos(2.0 * math.pi * step / span)
    s = math.sin(2.0 * math.pi * step / span)
    if (8 * step) % span == 0:
        r = abs(c)
        a, b = r * (re + im), r * (im - re)
        eighth = 8 * step // span
        return {1: (a, b), 3: (b, -a), 5: (-a, -b), 7: (-b, a)}[eighth]
    return (c * re + s * im, c * im - s * re)


def complex_dft(values, way):
    n = len(values)
    if n == 1:
        return values
    even = complex_dft(values[0::2], way)
    odd = complex_dft(values[1::2], way)
    out = [None] * n
    for k in range(n // 2):
        tr, ti = turn(odd[k], way * k, n)
        er, ei = even[k]
        out[k] = (er + tr, ei + ti)
        out[k + n // 2] = (er - tr, ei - ti)
    return out


def odd_bins(d, span):
    q = span // 4
    z = [turn((d[n], -d[n + q]), n, span) for n in range(q)]
    out = {}
    for m, (re, im) in enumerate(complex_dft(z, 1)):
        k = 4 * m + 1
        if k < span // 2:
            out[k] = (re, im)
        else:
            out[span - k] = (re, -im)
    return out


def real_bins(x):
    n = len(x)
    if n == 1:
        return {0: (x[0], None)}
    h = n // 2
    out = {2 * k: v for k, v in real_bins([x[i] + x[i + h] for i in range(h)]).items()}
    d = [x[i] - x[i + h] for i in range(h)]
    if n == 2:
        out[1] = (d[0], None)
    else:
        out.update(odd_bins(d, n))
    return out


def padded_bins(x):
    out = {2 * k: v for k, v in real_bins(x).items()}
    out.update(odd_bins(x, 2 * len(x)))
    return out


def odd_back(bins, span):
    q = span // 4
    c = []
    for m in range(q):
        k = 4 * m + 1
        if k < span // 2:
            c.append(bins[k])
        else:
            re, im = bins[span - k]
            c.append((re, -im))
    w = [turn(v, -n, span) for n, v in enumerate(complex_dft(c, -1))]
    return [v[0] for v in w] + [-v[1] for v in w]


def real_back(bins, n):
    if n == 1:
        return [bins[0][0]]
    if n == 2:
        return [bins[0][0] + bins[1][0], bins[0][0] - bins[1][0]]
    h = n // 2
    e = real_back({k // 2: bins[k] for k in bins if k % 2 == 0}, h)
    o = odd_back({k: bins[k] for k in bins if k % 2 == 1}, n)
    return [a + b for a, b in zip(e, o)] + [a - b for a, b in zip(e, o)]


def padded_back(bins, n):
    e = real_back({k // 2: bins[k] for k in bins if k % 2 == 0}, n)
    o = odd_back({k: bins[k] for k in bins if k % 2 == 1}, 2 * n)
    return [a + b for a, b in zip(e, o)]


def inner_tables(blocks):
    span = 2 * blocks
    full = span * TILE
    k1 = np.arange(blocks + 1).reshape(-1, 1, 1)
    k2 = np.arange(TILE).reshape(1, -1, 1)
    n2 = np.arange(TILE).reshape(1, 1, -1)
    angle = (n2 * (k1 + span * k2) % full) * (2.0 * math.pi / full)
    c, s = np.cos(angle), np.sin(angle)
    fwd = np.concatenate(
        [np.concatenate([c, s], 2), np.concatenate([-s, c], 2)], 1
    )
    weight = np.where((k1 == 0) | (k1 == blocks), 1.0, 2.0) / full
    inv = fwd.transpose(0, 2, 1) * weight

    return fwd.astype(ml_dtypes.bfloat16), inv.astype(ml_dtypes.bfloat16)


def fused_kernel(
    cfg,
    k_hbm, v_hbm, q_hbm, og_hbm, filt_hbm, fwd_hbm, inv_hbm,
    qg_hbm, kg_hbm, vg_hbm, raw_hbm, fac_ref,
    k_ref, v_ref, q_ref, og_ref, filt_ref, raw_ref, fwd, inv, send, recv, outer, spec_f, spec_kv, spec_gg, back, wide,
    sq_mine, sq_tp, sq_pair, sq_all,
    load_sem, store_sem, raw_sem, table_sem, send_sem, recv_sem, sq_send, sq_recv, tp_send, tp_recv,
):
    blocks, n_ctx, n_tp, entries = cfg
    me = lax.axis_index("blk") * n_ctx + lax.axis_index("ctx")
    my_tp = lax.axis_index("tp")
    bins = blocks + 1

    def place(d):
        return {"blk": d // n_ctx, "ctx": d % n_ctx}

    quarter = k_ref.shape[1] // 4

    def load(which, part):
        hbm, vmem = (
            (k_hbm, k_ref), (v_hbm, v_ref), (og_hbm, og_ref), (q_hbm, q_ref), (filt_hbm, filt_ref)
        )[which]
        cols = pl.ds(part * quarter, quarter)
        return pltpu.make_async_copy(
            hbm.at[:, cols], vmem.at[:, cols], load_sem.at[which, part]
        )

    for pair in ((0, 1), (2, 3), (4,)):
        for part in range(4):
            for which in pair:
                load(which, part).start()
    get_fwd = pltpu.make_async_copy(fwd_hbm, fwd, table_sem.at[0])
    get_inv = pltpu.make_async_copy(inv_hbm, inv, table_sem.at[1])
    get_fwd.start()
    get_inv.start()

    barrier = pltpu.get_barrier_semaphore()

    def greet(j, carry):
        d = lax.rem(me + j, blocks)
        pl.semaphore_signal(barrier, inc=1, device_id=place(d), device_id_type=MESH)
        return carry

    lax.fori_loop(1, blocks, greet, 0)
    for j in range(1, n_tp):
        pl.semaphore_signal(
            barrier, inc=1, device_id={"tp": lax.rem(my_tp + j, n_tp)}, device_id_type=MESH
        )

    def gate(phase, a_ref, b_ref):
        for d in range(blocks):
            if d % (blocks // 4) == 0:
                load(2 * phase, d // (blocks // 4)).wait()
                load(2 * phase + 1, d // (blocks // 4)).wait()
            cols = slice(d * TILE, (d + 1) * TILE)
            send[phase, d] = gated_product(a_ref[:, cols], b_ref[:, cols])
        recv[phase, me] = send[phase, me]

    def out_copy(phase, d):
        return pltpu.make_async_remote_copy(
            src_ref=send.at[phase, d],
            dst_ref=recv.at[phase, me],
            send_sem=send_sem.at[phase, d],
            recv_sem=recv_sem.at[phase, me],
            device_id=place(d),
            device_id_type=MESH,
        )

    def in_copy(phase, s):
        return pltpu.make_async_remote_copy(
            src_ref=send.at[phase, s],
            dst_ref=recv.at[phase, s],
            send_sem=send_sem.at[phase, s],
            recv_sem=recv_sem.at[phase, s],
            device_id=place(s),
            device_id_type=MESH,
        )

    def flipped(place_on_axis, mask):
        out, weight = 0, 1
        while weight < n_ctx:
            bit = lax.rem(place_on_axis // weight, 2)
            out = out + weight * (1 - bit if mask & weight else bit)
            weight *= 2
        return out

    def start_all(phase):
        masks = [m for pair in zip(range(n_ctx - 1, -1, -1), range(n_ctx)) for m in pair][:n_ctx]
        ctxs = [(mask, flipped(lax.axis_index("ctx"), mask)) for mask in masks]
        for j in range(blocks // n_ctx):
            blk = lax.rem(lax.axis_index("blk") + j, blocks // n_ctx)
            for mask, ctx in ctxs:
                if j or mask:
                    out_copy(phase, blk * n_ctx + ctx).start()

    def arrive_all(phase):
        def one(j, carry):
            in_copy(phase, lax.rem(me + blocks - j, blocks)).wait_recv()
            return carry

        lax.fori_loop(1, blocks, one, 0)

    def rows_at(i):
        return pl.ds(pl.multiple_of(i * CHUNK, CHUNK), CHUNK)

    def outer_forward(load):
        def one(i, carry):
            rows = rows_at(i)
            out = padded_bins([load(n, rows).astype(F32) for n in range(blocks)])
            low = pl.ds(pl.multiple_of(TILE + i * CHUNK, CHUNK), CHUNK)
            for k in range(bins):
                re, im = out[k]
                outer[k, rows, :] = re.astype(BF16)
                outer[k, low, :] = (jnp.zeros_like(re) if im is None else im).astype(BF16)
            return carry

        lax.fori_loop(0, TILE // CHUNK, one, 0)

    def apply(table, k, value):
        return jnp.dot(table[k], value, preferred_element_type=F32)

    def times(a, b, conjugate):
        ar, ai = a[:TILE], a[TILE:]
        br, bi = b[:TILE], b[TILE:]
        if conjugate:
            return jnp.concatenate([ar * br + ai * bi, ai * br - ar * bi], 0).astype(BF16)
        return jnp.concatenate([ar * br - ai * bi, ar * bi + ai * br], 0).astype(BF16)

    def outer_back(store):
        def one(i, carry):
            rows = rows_at(i)
            low = pl.ds(pl.multiple_of(TILE + i * CHUNK, CHUNK), CHUNK)
            got = {k: (back[k, rows, :], back[k, low, :]) for k in range(bins)}
            for n, y in enumerate(padded_back(got, blocks)):
                store(n, rows, y)
            return carry

        lax.fori_loop(0, TILE // CHUNK, one, 0)

    def store_send(phase):
        def store(n, rows, y):
            send[phase, n, rows, :] = y.astype(BF16)

        return store

    def store_wide(n, rows, y):
        wide[n, rows, :] = y

    gate(0, k_ref, v_ref)
    pl.semaphore_wait(barrier, blocks - 1 + n_tp - 1)
    start_all(0)
    gate(1, og_ref, q_ref)
    start_all(1)

    for part in range(4):
        load(4, part).wait()
    for n in range(blocks):
        wide[n] = filt_ref[:, n * TILE : (n + 1) * TILE].T
    outer_forward(lambda n, rows: wide[n, rows, :])
    get_fwd.wait()
    get_inv.wait()

    def each_bin(step):
        def group(i, carry):
            step([GROUP * i + g for g in range(GROUP)])
            return carry

        lax.fori_loop(0, bins // GROUP, group, 0)
        if bins % GROUP:
            step(list(range(bins - bins % GROUP, bins)))

    def filter_step(ks):
        specs = [apply(fwd, k, outer[k]) for k in ks]
        for k, spec in zip(ks, specs):
            spec_f[k] = spec

    each_bin(filter_step)

    arrive_all(0)
    outer_forward(lambda n, rows: recv[0, n, rows, :])

    def gated_step(ks):
        specs = [apply(fwd, k, outer[k]) for k in ks]
        products = [times(spec, spec_f[k], False) for k, spec in zip(ks, specs)]
        results = [apply(inv, k, product) for k, product in zip(ks, products)]
        for k, spec, result in zip(ks, specs, results):
            spec_kv[k] = spec
            back[k] = result

    each_bin(gated_step)
    outer_back(store_send(2))
    recv[2, me] = send[2, me]
    start_all(2)

    arrive_all(1)
    outer_forward(lambda n, rows: recv[1, n, rows, :])

    def gate_step(ks):
        specs = [apply(fwd, k, outer[k]) for k in ks]
        products = [times(spec, spec_f[k], True) for k, spec in zip(ks, specs)]
        results = [apply(inv, k, product) for k, product in zip(ks, products)]
        for k, spec, result in zip(ks, specs, results):
            spec_gg[k] = spec
            back[k] = result

    each_bin(gate_step)
    outer_back(store_send(3))
    recv[3, me] = send[3, me]
    start_all(3)

    def raw_step(ks):
        products = [times(spec_gg[k], spec_kv[k], True) for k in ks]
        results = [apply(inv, k, product) for k, product in zip(ks, products)]
        for k, result in zip(ks, results):
            back[k] = result

    each_bin(raw_step)
    outer_back(store_wide)
    total = jnp.zeros((8, TILE), F32)
    for n in range(blocks):
        tile = wide[n]
        raw_ref[:, n * TILE : (n + 1) * TILE] = tile.T
        total = total + jnp.sum((tile * tile).reshape(TILE // 8, 8, TILE), 0)
    put_raw = pltpu.make_async_copy(raw_ref, raw_hbm, raw_sem)
    put_raw.start()
    sq_mine[...] = total

    def tp_copy(j):
        return pltpu.make_async_remote_copy(
            src_ref=sq_mine,
            dst_ref=sq_tp.at[j - 1],
            send_sem=tp_send.at[j - 1],
            recv_sem=tp_recv.at[j - 1],
            device_id={"tp": lax.rem(my_tp + j, n_tp)},
            device_id_type=MESH,
        )

    for j in range(1, n_tp):
        tp_copy(j).start()
    for j in range(1, n_tp):
        tp_copy(j).wait()
        total = total + sq_tp[j - 1]
    sq_pair[...] = total
    sq_all[me] = total

    def sq_out(d):
        return pltpu.make_async_remote_copy(
            src_ref=sq_pair,
            dst_ref=sq_all.at[me],
            send_sem=sq_send.at[d],
            recv_sem=sq_recv.at[me],
            device_id=place(d),
            device_id_type=MESH,
        )

    def sq_in(s):
        return pltpu.make_async_remote_copy(
            src_ref=sq_pair,
            dst_ref=sq_all.at[s],
            send_sem=sq_send.at[s],
            recv_sem=sq_recv.at[s],
            device_id=place(s),
            device_id_type=MESH,
        )

    def sq_start(j, carry):
        sq_out(lax.rem(me + j, blocks)).start()
        return carry

    def sq_arrive(j, carry):
        sq_in(lax.rem(me + blocks - j, blocks)).wait_recv()
        return carry

    lax.fori_loop(1, blocks, sq_start, 0)

    def columns(s):
        return pl.ds(pl.multiple_of(s * TILE, TILE), TILE)

    def put(which, s):
        hbm, slot = ((qg_hbm, 2), (kg_hbm, 3), (vg_hbm, 0))[which]
        return pltpu.make_async_copy(
            recv.at[slot, s], hbm.at[:, columns(s)], store_sem.at[which, s]
        )

    def finish_query(s):
        recv[2, s] = gated_product(og_ref[:, columns(s)], recv[2, s])
        put(0, s).start()

    def finish_grad(s):
        grad = recv[3, s]
        recv[3, s] = gated_product(grad, v_ref[:, columns(s)])
        put(1, s).start()
        recv[0, s] = gated_product(grad, k_ref[:, columns(s)])
        put(2, s).start()

    def finish_all(phase, finish):
        finish(me)

        def one(j, carry):
            s = lax.rem(me + blocks - j, blocks)
            in_copy(phase, s).wait_recv()
            finish(s)
            return carry

        lax.fori_loop(1, blocks, one, 0)

    finish_all(2, finish_query)
    lax.fori_loop(1, blocks, sq_arrive, 0)
    mean = jnp.sum(jnp.sum(sq_all[...], 0), keepdims=True) / entries
    rms = jnp.sqrt(mean + 1e-06)
    fac_ref[...] = jnp.minimum(1.0, 1.0 / rms)
    finish_all(3, finish_grad)

    def stored(s, carry):
        for which in range(3):
            put(which, s).wait()
        return carry

    def sent(j, carry):
        d = lax.rem(me + j, blocks)
        for phase in range(4):
            out_copy(phase, d).wait_send()
        sq_out(d).wait_send()
        return carry

    lax.fori_loop(1, blocks, sent, 0)
    put_raw.wait()
    lax.fori_loop(0, blocks, stored, 0)


def finish_kernel(
    qg_in, kg_in, vg_in, raw_hbm, fac_ref, qg_out, kg_out, vg_out, fg_hbm,
    qg, kg, vg, raw, load_sem, store_sem,
):
    step = raw.shape[0] // PARTS

    def copy(src, dst, sems, i, part):
        rows = pl.ds(part * step, step)
        return pltpu.make_async_copy(src.at[rows], dst.at[rows], sems.at[i, part])

    ways = ((raw_hbm, raw, fg_hbm), (qg_in, qg, qg_out), (kg_in, kg, kg_out), (vg_in, vg, vg_out))
    for part in range(PARTS):
        for i, (src, held, dst) in enumerate(ways):
            copy(src, held, load_sem, i, part).start()
    for part in range(PARTS):
        for i, (src, held, dst) in enumerate(ways):
            copy(src, held, load_sem, i, part).wait()
            if i == 0:
                rows = slice(part * step, (part + 1) * step)
                raw[rows] = raw[rows] * fac_ref[...]
            copy(held, dst, store_sem, i, part).start()
    for part in range(PARTS):
        for i, (src, held, dst) in enumerate(ways):
            copy(held, dst, store_sem, i, part).wait()


def fused_body(mesh, query_proj, key_proj, value_proj, output_grad, long_filter):
    n_blk, n_ctx, n_tp = mesh.shape["blk"], mesh.shape["ctx"], mesh.shape["tp"]
    blocks = n_blk * n_ctx
    bins = blocks + 1
    tokens, width = query_proj.shape
    chan_count, seq_length = long_filter.shape[1:]
    entries = float(chan_count * seq_length * blocks * n_tp)
    fwd, inv = inner_tables(blocks)
    vmem = pl.BlockSpec(memory_space=pltpu.VMEM)
    hbm = pl.BlockSpec(memory_space=pltpu.HBM)
    stream = pltpu.VMEM((tokens, width), BF16)
    lags = pltpu.VMEM((chan_count, seq_length), F32)
    dma = pltpu.SemaphoreType.DMA
    spec = pltpu.VMEM((bins, 2 * TILE, TILE), F32)
    rows_like = jax.ShapeDtypeStruct((tokens, width), BF16)
    flops = 6 * bins * 2 * 2 * TILE * 2 * TILE * TILE
    query_part, key_part, value_part, filter_raw, factor = pl.pallas_call(
        functools.partial(fused_kernel, (blocks, n_ctx, n_tp, entries)),
        out_shape=(
            rows_like, rows_like, rows_like,
            jax.ShapeDtypeStruct((chan_count, seq_length), F32),
            jax.ShapeDtypeStruct((1, 1), F32),
        ),
        in_specs=[hbm] * 7,
        out_specs=(hbm, hbm, hbm, hbm, vmem),
        scratch_shapes=[
            stream, stream, stream, stream, lags, lags,
            pltpu.VMEM(fwd.shape, BF16),
            pltpu.VMEM(inv.shape, BF16),
            pltpu.VMEM((4, blocks, TILE, TILE), BF16),
            pltpu.VMEM((4, blocks, TILE, TILE), BF16),
            pltpu.VMEM((bins, 2 * TILE, TILE), BF16),
            spec, spec, spec, spec,
            pltpu.VMEM((blocks, TILE, TILE), F32),
            pltpu.VMEM((8, TILE), F32),
            pltpu.VMEM((max(n_tp - 1, 1), 8, TILE), F32),
            pltpu.VMEM((8, TILE), F32),
            pltpu.VMEM((blocks, 8, TILE), F32),
            dma((5, 4)),
            dma((3, blocks)),
            dma(()),
            dma((2,)),
            dma((4, blocks)),
            dma((4, blocks)),
            dma((blocks,)),
            dma((blocks,)),
            dma((max(n_tp - 1, 1),)),
            dma((max(n_tp - 1, 1),)),
        ],
        compiler_params=pltpu.CompilerParams(
            collective_id=0, has_side_effects=True, vmem_limit_bytes=VMEM_LIMIT
        ),
        cost_estimate=pl.CostEstimate(
            flops=flops, bytes_accessed=16 * tokens * width, transcendentals=0
        ),
    )(
        key_proj, value_proj, query_proj, output_grad,
        long_filter.reshape(chan_count, seq_length),
        jnp.asarray(fwd), jnp.asarray(inv),
    )
    query_grad, key_grad, value_grad, filter_grad = pl.pallas_call(
        finish_kernel,
        out_shape=(rows_like,) * 3 + (jax.ShapeDtypeStruct((chan_count, seq_length), F32),),
        in_specs=[hbm] * 4 + [vmem],
        out_specs=(hbm,) * 4,
        scratch_shapes=[stream, stream, stream, lags, dma((4, PARTS)), dma((4, PARTS))],
        compiler_params=pltpu.CompilerParams(vmem_limit_bytes=VMEM_LIMIT),
        cost_estimate=pl.CostEstimate(
            flops=tokens * width, bytes_accessed=20 * tokens * width, transcendentals=0
        ),
    )(query_part, key_part, value_part, filter_raw, factor)
    filter_grad = filter_grad.reshape(1, chan_count, seq_length)
    return (query_grad, key_grad, value_grad, filter_grad)


def general_body(query_proj, key_proj, value_proj, output_grad, long_filter):
    axes = ("blk", "ctx")
    chan_count = long_filter.shape[1]
    seq_length = long_filter.shape[2]
    kernel_cols = long_filter.reshape(chan_count, seq_length)

    def to_channels(rows):
        return lax.all_to_all(rows.T, axes, split_axis=0, concat_axis=1, tiled=True)

    def to_tokens(cols):
        return lax.all_to_all(cols, axes, split_axis=1, concat_axis=0, tiled=True).T

    gated_cols = to_channels(gated_product(key_proj, value_proj))
    gate_cols = to_channels(gated_product(output_grad, query_proj))
    conv_out, conv_grad, filter_raw = channel_work(gated_cols, gate_cols, kernel_cols)
    conv_out, conv_grad = to_tokens(conv_out), to_tokens(conv_grad)
    query_grad = gated_product(output_grad, conv_out)
    key_grad = gated_product(conv_grad, value_proj)
    value_grad = gated_product(conv_grad, key_proj)
    square_total = lax.psum(jnp.sum(filter_raw * filter_raw), ("blk", "ctx", "tp"))
    entry_count = (
        chan_count * seq_length * lax.axis_size("blk") * lax.axis_size("ctx") * lax.axis_size("tp")
    )
    grad_rms = jnp.sqrt(square_total / entry_count + 1e-06)
    factor = jnp.minimum(1.0, 1.0 / grad_rms)
    filter_grad = (filter_raw * factor).reshape(1, chan_count, seq_length)
    return (query_grad, key_grad, value_grad, filter_grad)


def body(mesh, *args):
    blocks = mesh.shape["blk"] * mesh.shape["ctx"]
    fits = args[0].shape[0] == TILE and args[4].shape[1] == TILE and blocks in (4, 8, 16)
    if fits:
        return fused_body(mesh, *args)
    return general_body(*args)


def solution(mesh):
    in_specs = (
        P(("blk", "ctx"), "tp"),
        P(("blk", "ctx"), "tp"),
        P(("blk", "ctx"), "tp"),
        P(("blk", "ctx"), "tp"),
        P("tp", ("blk", "ctx"), None),
    )
    out_specs = (
        P(("blk", "ctx"), "tp"),
        P(("blk", "ctx"), "tp"),
        P(("blk", "ctx"), "tp"),
        P("tp", ("blk", "ctx"), None),
    )
    return jax.shard_map(
        functools.partial(body, mesh), mesh=mesh, in_specs=in_specs, out_specs=out_specs, check_vma=False
    )
```

```python
import functools
import math

import jax
import jax.numpy as jnp
import ml_dtypes
import numpy as np
from jax import lax
from jax.experimental import pallas as pl
from jax.experimental.pallas import tpu as pltpu
from jax.sharding import PartitionSpec as P

PRECISE = lax.Precision.HIGH
MESH = pl.DeviceIdType.MESH
TILE = 128
PARTS = 4
CHUNK = 16
GROUP = 4
VMEM_LIMIT = 63 * 1024 * 1024
F32 = jnp.float32
BF16 = jnp.bfloat16


def spectrum_tables(seq_length):
    outer_size = seq_length // 64
    half_size = outer_size // 2
    full_size = outer_size * 128
    row_index = lax.broadcasted_iota(jnp.int32, (outer_size, half_size), 0)
    col_index = lax.broadcasted_iota(jnp.int32, (outer_size, half_size), 1)
    outer_angle = (row_index * col_index % outer_size).astype(jnp.float32) * (
        2.0 * math.pi / outer_size
    )
    inner_row = lax.broadcasted_iota(jnp.int32, (128, 128), 0)
    inner_col = lax.broadcasted_iota(jnp.int32, (128, 128), 1)
    inner_angle = (inner_row * inner_col % 128).astype(jnp.float32) * (2.0 * math.pi / 128)
    twist_row = lax.broadcasted_iota(jnp.int32, (outer_size, 128), 0)
    twist_col = lax.broadcasted_iota(jnp.int32, (outer_size, 128), 1)
    twist_angle = (twist_row * twist_col % full_size).astype(jnp.float32) * (
        2.0 * math.pi / full_size
    )
    return (
        jnp.cos(outer_angle),
        jnp.sin(outer_angle),
        jnp.cos(inner_angle),
        jnp.sin(inner_angle),
        jnp.cos(twist_angle),
        jnp.sin(twist_angle),
        full_size,
    )


def to_spectrum(signal, tables):
    outer_cos, outer_sin, inner_cos, inner_sin, twist_cos, twist_sin, full_size = tables
    blocks = signal.reshape(signal.shape[0], outer_cos.shape[1], 128)
    first_real = jnp.einsum("kn,cnm->ckm", outer_cos, blocks, precision=PRECISE)
    first_imag = -jnp.einsum("kn,cnm->ckm", outer_sin, blocks, precision=PRECISE)
    turned_real = first_real * twist_cos + first_imag * twist_sin
    turned_imag = first_imag * twist_cos - first_real * twist_sin
    real_part = jnp.einsum("ckm,mj->ckj", turned_real, inner_cos, precision=PRECISE) + jnp.einsum(
        "ckm,mj->ckj", turned_imag, inner_sin, precision=PRECISE
    )
    imag_part = jnp.einsum("ckm,mj->ckj", turned_imag, inner_cos, precision=PRECISE) - jnp.einsum(
        "ckm,mj->ckj", turned_real, inner_sin, precision=PRECISE
    )
    return (real_part, imag_part)


def from_spectrum(spectrum, tables):
    outer_cos, outer_sin, inner_cos, inner_sin, twist_cos, twist_sin, full_size = tables
    real_part, imag_part = spectrum
    mixed_real = jnp.einsum("ckm,mj->ckj", real_part, inner_cos, precision=PRECISE) - jnp.einsum(
        "ckm,mj->ckj", imag_part, inner_sin, precision=PRECISE
    )
    mixed_imag = jnp.einsum("ckm,mj->ckj", imag_part, inner_cos, precision=PRECISE) + jnp.einsum(
        "ckm,mj->ckj", real_part, inner_sin, precision=PRECISE
    )
    turned_real = mixed_real * twist_cos - mixed_imag * twist_sin
    turned_imag = mixed_imag * twist_cos + mixed_real * twist_sin
    signal = jnp.einsum("kn,ckm->cnm", outer_cos, turned_real, precision=PRECISE) - jnp.einsum(
        "kn,ckm->cnm", outer_sin, turned_imag, precision=PRECISE
    )
    return (signal / full_size).reshape(signal.shape[0], -1)


def complex_product(left, right, conjugate):
    left_real, left_imag = left
    right_real, right_imag = right
    if conjugate:
        return (
            left_real * right_real + left_imag * right_imag,
            left_imag * right_real - left_real * right_imag,
        )
    return (
        left_real * right_real - left_imag * right_imag,
        left_real * right_imag + left_imag * right_real,
    )


def channel_work(gated_cols, gate_cols, kernel_cols):
    tables = spectrum_tables(kernel_cols.shape[1])
    kernel_spec = to_spectrum(kernel_cols, tables)
    gated_spec = to_spectrum(gated_cols.astype(jnp.float32), tables)
    gate_spec = to_spectrum(gate_cols.astype(jnp.float32), tables)
    conv_out = from_spectrum(complex_product(gated_spec, kernel_spec, False), tables).astype(
        jnp.bfloat16
    )
    conv_grad = from_spectrum(complex_product(gate_spec, kernel_spec, True), tables).astype(
        jnp.bfloat16
    )
    filter_raw = from_spectrum(complex_product(gate_spec, gated_spec, True), tables)
    return (conv_out, conv_grad, filter_raw)


def gated_product(left, right):
    return (left.astype(jnp.float32) * right.astype(jnp.float32)).astype(jnp.bfloat16)


def turn(value, step, span):
    re, im = value
    step = step % span
    if step == 0:
        return value
    if 4 * step == span:
        return (im, -re)
    if 2 * step == span:
        return (-re, -im)
    if 4 * step == 3 * span:
        return (-im, re)
    c = math.cos(2.0 * math.pi * step / span)
    s = math.sin(2.0 * math.pi * step / span)
    if (8 * step) % span == 0:
        r = abs(c)
        a, b = r * (re + im), r * (im - re)
        eighth = 8 * step // span
        return {1: (a, b), 3: (b, -a), 5: (-a, -b), 7: (-b, a)}[eighth]
    return (c * re + s * im, c * im - s * re)


def complex_dft(values, way):
    n = len(values)
    if n == 1:
        return values
    even = complex_dft(values[0::2], way)
    odd = complex_dft(values[1::2], way)
    out = [None] * n
    for k in range(n // 2):
        tr, ti = turn(odd[k], way * k, n)
        er, ei = even[k]
        out[k] = (er + tr, ei + ti)
        out[k + n // 2] = (er - tr, ei - ti)
    return out


def odd_bins(d, span):
    q = span // 4
    z = [turn((d[n], -d[n + q]), n, span) for n in range(q)]
    out = {}
    for m, (re, im) in enumerate(complex_dft(z, 1)):
        k = 4 * m + 1
        if k < span // 2:
            out[k] = (re, im)
        else:
            out[span - k] = (re, -im)
    return out


def real_bins(x):
    n = len(x)
    if n == 1:
        return {0: (x[0], None)}
    h = n // 2
    out = {2 * k: v for k, v in real_bins([x[i] + x[i + h] for i in range(h)]).items()}
    d = [x[i] - x[i + h] for i in range(h)]
    if n == 2:
        out[1] = (d[0], None)
    else:
        out.update(odd_bins(d, n))
    return out


def padded_bins(x):
    out = {2 * k: v for k, v in real_bins(x).items()}
    out.update(odd_bins(x, 2 * len(x)))
    return out


def odd_back(bins, span):
    q = span // 4
    c = []
    for m in range(q):
        k = 4 * m + 1
        if k < span // 2:
            c.append(bins[k])
        else:
            re, im = bins[span - k]
            c.append((re, -im))
    w = [turn(v, -n, span) for n, v in enumerate(complex_dft(c, -1))]
    return [v[0] for v in w] + [-v[1] for v in w]


def real_back(bins, n):
    if n == 1:
        return [bins[0][0]]
    if n == 2:
        return [bins[0][0] + bins[1][0], bins[0][0] - bins[1][0]]
    h = n // 2
    e = real_back({k // 2: bins[k] for k in bins if k % 2 == 0}, h)
    o = odd_back({k: bins[k] for k in bins if k % 2 == 1}, n)
    return [a + b for a, b in zip(e, o)] + [a - b for a, b in zip(e, o)]


def padded_back(bins, n):
    e = real_back({k // 2: bins[k] for k in bins if k % 2 == 0}, n)
    o = odd_back({k: bins[k] for k in bins if k % 2 == 1}, 2 * n)
    return [a + b for a, b in zip(e, o)]


def inner_tables(blocks):
    span = 2 * blocks
    full = span * TILE
    k1 = np.arange(blocks + 1).reshape(-1, 1, 1)
    k2 = np.arange(TILE).reshape(1, -1, 1)
    n2 = np.arange(TILE).reshape(1, 1, -1)
    angle = (n2 * (k1 + span * k2) % full) * (2.0 * math.pi / full)
    c, s = np.cos(angle), np.sin(angle)
    fwd = np.concatenate(
        [np.concatenate([c, s], 2), np.concatenate([-s, c], 2)], 1
    )
    weight = np.where((k1 == 0) | (k1 == blocks), 1.0, 2.0) / full
    inv = fwd.transpose(0, 2, 1) * weight

    return fwd.astype(ml_dtypes.bfloat16), inv.astype(ml_dtypes.bfloat16)


def fused_kernel(
    cfg,
    k_hbm, v_hbm, q_hbm, og_hbm, filt_hbm, fwd_hbm, inv_hbm,
    qg_hbm, kg_hbm, vg_hbm, raw_hbm, fac_ref,
    k_ref, v_ref, q_ref, og_ref, filt_ref, raw_ref, fwd, inv, send, recv, outer, spec_f, spec_kv, spec_gg, back, wide,
    sq_mine, sq_tp, sq_pair, sq_all,
    load_sem, store_sem, raw_sem, table_sem, send_sem, recv_sem, sq_send, sq_recv, tp_send, tp_recv,
):
    blocks, n_ctx, n_tp, entries = cfg
    me = lax.axis_index("blk") * n_ctx + lax.axis_index("ctx")
    my_tp = lax.axis_index("tp")
    bins = blocks + 1

    def place(d):
        return {"blk": d // n_ctx, "ctx": d % n_ctx}

    quarter = k_ref.shape[1] // 4

    def load(which, part):
        hbm, vmem = (
            (k_hbm, k_ref), (v_hbm, v_ref), (og_hbm, og_ref), (q_hbm, q_ref), (filt_hbm, filt_ref)
        )[which]
        cols = pl.ds(part * quarter, quarter)
        return pltpu.make_async_copy(
            hbm.at[:, cols], vmem.at[:, cols], load_sem.at[which, part]
        )

    for pair in ((0, 1), (2, 3), (4,)):
        for part in range(4):
            for which in pair:
                load(which, part).start()
    get_fwd = pltpu.make_async_copy(fwd_hbm, fwd, table_sem.at[0])
    get_inv = pltpu.make_async_copy(inv_hbm, inv, table_sem.at[1])
    get_fwd.start()
    get_inv.start()

    barrier = pltpu.get_barrier_semaphore()

    def greet(j, carry):
        d = lax.rem(me + j, blocks)
        pl.semaphore_signal(barrier, inc=1, device_id=place(d), device_id_type=MESH)
        return carry

    lax.fori_loop(1, blocks, greet, 0)
    for j in range(1, n_tp):
        pl.semaphore_signal(
            barrier, inc=1, device_id={"tp": lax.rem(my_tp + j, n_tp)}, device_id_type=MESH
        )

    def gate(phase, a_ref, b_ref):
        for d in range(blocks):
            if d % (blocks // 4) == 0:
                load(2 * phase, d // (blocks // 4)).wait()
                load(2 * phase + 1, d // (blocks // 4)).wait()
            cols = slice(d * TILE, (d + 1) * TILE)
            send[phase, d] = gated_product(a_ref[:, cols], b_ref[:, cols])
        recv[phase, me] = send[phase, me]

    def out_copy(phase, d):
        return pltpu.make_async_remote_copy(
            src_ref=send.at[phase, d],
            dst_ref=recv.at[phase, me],
            send_sem=send_sem.at[phase, d],
            recv_sem=recv_sem.at[phase, me],
            device_id=place(d),
            device_id_type=MESH,
        )

    def in_copy(phase, s):
        return pltpu.make_async_remote_copy(
            src_ref=send.at[phase, s],
            dst_ref=recv.at[phase, s],
            send_sem=send_sem.at[phase, s],
            recv_sem=recv_sem.at[phase, s],
            device_id=place(s),
            device_id_type=MESH,
        )

    def flipped(place_on_axis, mask):
        out, weight = 0, 1
        while weight < n_ctx:
            bit = lax.rem(place_on_axis // weight, 2)
            out = out + weight * (1 - bit if mask & weight else bit)
            weight *= 2
        return out

    def start_all(phase):
        masks = [m for pair in zip(range(n_ctx - 1, -1, -1), range(n_ctx)) for m in pair][:n_ctx]
        ctxs = [(mask, flipped(lax.axis_index("ctx"), mask)) for mask in masks]
        for j in range(blocks // n_ctx):
            blk = lax.rem(lax.axis_index("blk") + j, blocks // n_ctx)
            for mask, ctx in ctxs:
                if j or mask:
                    out_copy(phase, blk * n_ctx + ctx).start()

    def arrive_all(phase):
        def one(j, carry):
            in_copy(phase, lax.rem(me + blocks - j, blocks)).wait_recv()
            return carry

        lax.fori_loop(1, blocks, one, 0)

    def rows_at(i):
        return pl.ds(pl.multiple_of(i * CHUNK, CHUNK), CHUNK)

    def outer_forward(load):
        def one(i, carry):
            rows = rows_at(i)
            tiles = [load(n, rows).astype(F32) for n in range(blocks)]
            halves = [padded_bins([t[h : h + 8] for t in tiles]) for h in (0, 8)]
            low = pl.ds(pl.multiple_of(TILE + i * CHUNK, CHUNK), CHUNK)
            for k in range(bins):
                re, im = zip(*[half[k] for half in halves])
                outer[k, rows, :] = jnp.concatenate(re, 0).astype(BF16)
                if im[0] is None:
                    outer[k, low, :] = jnp.zeros((CHUNK, TILE), BF16)
                else:
                    outer[k, low, :] = jnp.concatenate(im, 0).astype(BF16)
            return carry

        lax.fori_loop(0, TILE // CHUNK, one, 0)

    def apply(table, k, value):
        return jnp.dot(table[k], value, preferred_element_type=F32)

    def times(a, b, conjugate):
        ar, ai = a[:TILE], a[TILE:]
        br, bi = b[:TILE], b[TILE:]
        if conjugate:
            return jnp.concatenate([ar * br + ai * bi, ai * br - ar * bi], 0).astype(BF16)
        return jnp.concatenate([ar * br - ai * bi, ar * bi + ai * br], 0).astype(BF16)

    def outer_back(store):
        def one(i, carry):
            rows = rows_at(i)
            halves = []
            for h in (0, 8):
                top = pl.ds(pl.multiple_of(i * CHUNK + h, 8), 8)
                low = pl.ds(pl.multiple_of(TILE + i * CHUNK + h, 8), 8)
                got = {k: (back[k, top, :], back[k, low, :]) for k in range(bins)}
                halves.append(padded_back(got, blocks))
            for n, pair in enumerate(zip(*halves)):
                store(n, rows, jnp.concatenate(pair, 0))
            return carry

        lax.fori_loop(0, TILE // CHUNK, one, 0)

    def store_send(phase):
        def store(n, rows, y):
            send[phase, n, rows, :] = y.astype(BF16)

        return store

    def store_wide(n, rows, y):
        wide[n, rows, :] = y

    gate(0, k_ref, v_ref)
    pl.semaphore_wait(barrier, blocks - 1 + n_tp - 1)
    start_all(0)
    gate(1, og_ref, q_ref)
    start_all(1)

    for part in range(4):
        load(4, part).wait()
    for n in range(blocks):
        wide[n] = filt_ref[:, n * TILE : (n + 1) * TILE].T
    outer_forward(lambda n, rows: wide[n, rows, :])
    get_fwd.wait()
    get_inv.wait()

    def each_bin(step):
        def group(i, carry):
            step([GROUP * i + g for g in range(GROUP)])
            return carry

        lax.fori_loop(0, bins // GROUP, group, 0)
        if bins % GROUP:
            step(list(range(bins - bins % GROUP, bins)))

    def filter_step(ks):
        specs = [apply(fwd, k, outer[k]) for k in ks]
        for k, spec in zip(ks, specs):
            spec_f[k] = spec

    each_bin(filter_step)

    arrive_all(0)
    outer_forward(lambda n, rows: recv[0, n, rows, :])

    def gated_step(ks):
        specs = [apply(fwd, k, outer[k]) for k in ks]
        products = [times(spec, spec_f[k], False) for k, spec in zip(ks, specs)]
        results = [apply(inv, k, product) for k, product in zip(ks, products)]
        for k, spec, result in zip(ks, specs, results):
            spec_kv[k] = spec
            back[k] = result

    each_bin(gated_step)
    outer_back(store_send(2))
    recv[2, me] = send[2, me]
    start_all(2)

    arrive_all(1)
    outer_forward(lambda n, rows: recv[1, n, rows, :])

    def gate_step(ks):
        specs = [apply(fwd, k, outer[k]) for k in ks]
        products = [times(spec, spec_f[k], True) for k, spec in zip(ks, specs)]
        results = [apply(inv, k, product) for k, product in zip(ks, products)]
        for k, spec, result in zip(ks, specs, results):
            spec_gg[k] = spec
            back[k] = result

    each_bin(gate_step)
    outer_back(store_send(3))
    recv[3, me] = send[3, me]
    start_all(3)

    def raw_step(ks):
        products = [times(spec_gg[k], spec_kv[k], True) for k in ks]
        results = [apply(inv, k, product) for k, product in zip(ks, products)]
        for k, result in zip(ks, results):
            back[k] = result

    each_bin(raw_step)
    outer_back(store_wide)
    total = jnp.zeros((8, TILE), F32)
    for n in range(blocks):
        tile = wide[n]
        raw_ref[:, n * TILE : (n + 1) * TILE] = tile.T
        total = total + jnp.sum((tile * tile).reshape(TILE // 8, 8, TILE), 0)
    put_raw = pltpu.make_async_copy(raw_ref, raw_hbm, raw_sem)
    put_raw.start()
    sq_mine[...] = total

    def tp_copy(j):
        return pltpu.make_async_remote_copy(
            src_ref=sq_mine,
            dst_ref=sq_tp.at[j - 1],
            send_sem=tp_send.at[j - 1],
            recv_sem=tp_recv.at[j - 1],
            device_id={"tp": lax.rem(my_tp + j, n_tp)},
            device_id_type=MESH,
        )

    for j in range(1, n_tp):
        tp_copy(j).start()
    for j in range(1, n_tp):
        tp_copy(j).wait()
        total = total + sq_tp[j - 1]
    sq_pair[...] = total
    sq_all[me] = total

    def sq_out(d):
        return pltpu.make_async_remote_copy(
            src_ref=sq_pair,
            dst_ref=sq_all.at[me],
            send_sem=sq_send.at[d],
            recv_sem=sq_recv.at[me],
            device_id=place(d),
            device_id_type=MESH,
        )

    def sq_in(s):
        return pltpu.make_async_remote_copy(
            src_ref=sq_pair,
            dst_ref=sq_all.at[s],
            send_sem=sq_send.at[s],
            recv_sem=sq_recv.at[s],
            device_id=place(s),
            device_id_type=MESH,
        )

    def sq_start(j, carry):
        sq_out(lax.rem(me + j, blocks)).start()
        return carry

    def sq_arrive(j, carry):
        sq_in(lax.rem(me + blocks - j, blocks)).wait_recv()
        return carry

    lax.fori_loop(1, blocks, sq_start, 0)

    def columns(s):
        return pl.ds(pl.multiple_of(s * TILE, TILE), TILE)

    def put(which, s):
        hbm, slot = ((qg_hbm, 2), (kg_hbm, 3), (vg_hbm, 0))[which]
        return pltpu.make_async_copy(
            recv.at[slot, s], hbm.at[:, columns(s)], store_sem.at[which, s]
        )

    def finish_query(s):
        recv[2, s] = gated_product(og_ref[:, columns(s)], recv[2, s])
        put(0, s).start()

    def finish_grad(s):
        grad = recv[3, s]
        recv[3, s] = gated_product(grad, v_ref[:, columns(s)])
        put(1, s).start()
        recv[0, s] = gated_product(grad, k_ref[:, columns(s)])
        put(2, s).start()

    def finish_all(phase, finish):
        finish(me)

        def one(j, carry):
            s = lax.rem(me + blocks - j, blocks)
            in_copy(phase, s).wait_recv()
            finish(s)
            return carry

        lax.fori_loop(1, blocks, one, 0)

    finish_all(2, finish_query)
    lax.fori_loop(1, blocks, sq_arrive, 0)
    mean = jnp.sum(jnp.sum(sq_all[...], 0), keepdims=True) / entries
    rms = jnp.sqrt(mean + 1e-06)
    fac_ref[...] = jnp.minimum(1.0, 1.0 / rms)
    finish_all(3, finish_grad)

    def stored(s, carry):
        for which in range(3):
            put(which, s).wait()
        return carry

    def sent(j, carry):
        d = lax.rem(me + j, blocks)
        for phase in range(4):
            out_copy(phase, d).wait_send()
        sq_out(d).wait_send()
        return carry

    lax.fori_loop(1, blocks, sent, 0)
    put_raw.wait()
    lax.fori_loop(0, blocks, stored, 0)


def finish_kernel(
    qg_in, kg_in, vg_in, raw_hbm, fac_ref, qg_out, kg_out, vg_out, fg_hbm,
    qg, kg, vg, raw, load_sem, store_sem,
):
    step = raw.shape[0] // PARTS

    def copy(src, dst, sems, i, part):
        rows = pl.ds(part * step, step)
        return pltpu.make_async_copy(src.at[rows], dst.at[rows], sems.at[i, part])

    ways = ((raw_hbm, raw, fg_hbm), (qg_in, qg, qg_out), (kg_in, kg, kg_out), (vg_in, vg, vg_out))
    for part in range(PARTS):
        for i, (src, held, dst) in enumerate(ways):
            copy(src, held, load_sem, i, part).start()
    for part in range(PARTS):
        for i, (src, held, dst) in enumerate(ways):
            copy(src, held, load_sem, i, part).wait()
            if i == 0:
                rows = slice(part * step, (part + 1) * step)
                raw[rows] = raw[rows] * fac_ref[...]
            copy(held, dst, store_sem, i, part).start()
    for part in range(PARTS):
        for i, (src, held, dst) in enumerate(ways):
            copy(held, dst, store_sem, i, part).wait()


def fused_body(mesh, query_proj, key_proj, value_proj, output_grad, long_filter):
    n_blk, n_ctx, n_tp = mesh.shape["blk"], mesh.shape["ctx"], mesh.shape["tp"]
    blocks = n_blk * n_ctx
    bins = blocks + 1
    tokens, width = query_proj.shape
    chan_count, seq_length = long_filter.shape[1:]
    entries = float(chan_count * seq_length * blocks * n_tp)
    fwd, inv = inner_tables(blocks)
    vmem = pl.BlockSpec(memory_space=pltpu.VMEM)
    hbm = pl.BlockSpec(memory_space=pltpu.HBM)
    stream = pltpu.VMEM((tokens, width), BF16)
    lags = pltpu.VMEM((chan_count, seq_length), F32)
    dma = pltpu.SemaphoreType.DMA
    spec = pltpu.VMEM((bins, 2 * TILE, TILE), F32)
    rows_like = jax.ShapeDtypeStruct((tokens, width), BF16)
    flops = 6 * bins * 2 * 2 * TILE * 2 * TILE * TILE
    query_part, key_part, value_part, filter_raw, factor = pl.pallas_call(
        functools.partial(fused_kernel, (blocks, n_ctx, n_tp, entries)),
        out_shape=(
            rows_like, rows_like, rows_like,
            jax.ShapeDtypeStruct((chan_count, seq_length), F32),
            jax.ShapeDtypeStruct((1, 1), F32),
        ),
        in_specs=[hbm] * 7,
        out_specs=(hbm, hbm, hbm, hbm, vmem),
        scratch_shapes=[
            stream, stream, stream, stream, lags, lags,
            pltpu.VMEM(fwd.shape, BF16),
            pltpu.VMEM(inv.shape, BF16),
            pltpu.VMEM((4, blocks, TILE, TILE), BF16),
            pltpu.VMEM((4, blocks, TILE, TILE), BF16),
            pltpu.VMEM((bins, 2 * TILE, TILE), BF16),
            spec, spec, spec, spec,
            pltpu.VMEM((blocks, TILE, TILE), F32),
            pltpu.VMEM((8, TILE), F32),
            pltpu.VMEM((max(n_tp - 1, 1), 8, TILE), F32),
            pltpu.VMEM((8, TILE), F32),
            pltpu.VMEM((blocks, 8, TILE), F32),
            dma((5, 4)),
            dma((3, blocks)),
            dma(()),
            dma((2,)),
            dma((4, blocks)),
            dma((4, blocks)),
            dma((blocks,)),
            dma((blocks,)),
            dma((max(n_tp - 1, 1),)),
            dma((max(n_tp - 1, 1),)),
        ],
        compiler_params=pltpu.CompilerParams(
            collective_id=0, has_side_effects=True, vmem_limit_bytes=VMEM_LIMIT
        ),
        cost_estimate=pl.CostEstimate(
            flops=flops, bytes_accessed=16 * tokens * width, transcendentals=0
        ),
    )(
        key_proj, value_proj, query_proj, output_grad,
        long_filter.reshape(chan_count, seq_length),
        jnp.asarray(fwd), jnp.asarray(inv),
    )
    query_grad, key_grad, value_grad, filter_grad = pl.pallas_call(
        finish_kernel,
        out_shape=(rows_like,) * 3 + (jax.ShapeDtypeStruct((chan_count, seq_length), F32),),
        in_specs=[hbm] * 4 + [vmem],
        out_specs=(hbm,) * 4,
        scratch_shapes=[stream, stream, stream, lags, dma((4, PARTS)), dma((4, PARTS))],
        compiler_params=pltpu.CompilerParams(vmem_limit_bytes=VMEM_LIMIT),
        cost_estimate=pl.CostEstimate(
            flops=tokens * width, bytes_accessed=20 * tokens * width, transcendentals=0
        ),
    )(query_part, key_part, value_part, filter_raw, factor)
    filter_grad = filter_grad.reshape(1, chan_count, seq_length)
    return (query_grad, key_grad, value_grad, filter_grad)


def general_body(query_proj, key_proj, value_proj, output_grad, long_filter):
    axes = ("blk", "ctx")
    chan_count = long_filter.shape[1]
    seq_length = long_filter.shape[2]
    kernel_cols = long_filter.reshape(chan_count, seq_length)

    def to_channels(rows):
        return lax.all_to_all(rows.T, axes, split_axis=0, concat_axis=1, tiled=True)

    def to_tokens(cols):
        return lax.all_to_all(cols, axes, split_axis=1, concat_axis=0, tiled=True).T

    gated_cols = to_channels(gated_product(key_proj, value_proj))
    gate_cols = to_channels(gated_product(output_grad, query_proj))
    conv_out, conv_grad, filter_raw = channel_work(gated_cols, gate_cols, kernel_cols)
    conv_out, conv_grad = to_tokens(conv_out), to_tokens(conv_grad)
    query_grad = gated_product(output_grad, conv_out)
    key_grad = gated_product(conv_grad, value_proj)
    value_grad = gated_product(conv_grad, key_proj)
    square_total = lax.psum(jnp.sum(filter_raw * filter_raw), ("blk", "ctx", "tp"))
    entry_count = (
        chan_count * seq_length * lax.axis_size("blk") * lax.axis_size("ctx") * lax.axis_size("tp")
    )
    grad_rms = jnp.sqrt(square_total / entry_count + 1e-06)
    factor = jnp.minimum(1.0, 1.0 / grad_rms)
    filter_grad = (filter_raw * factor).reshape(1, chan_count, seq_length)
    return (query_grad, key_grad, value_grad, filter_grad)


def body(mesh, *args):
    blocks = mesh.shape["blk"] * mesh.shape["ctx"]
    fits = args[0].shape[0] == TILE and args[4].shape[1] == TILE and blocks in (4, 8, 16)
    if fits:
        return fused_body(mesh, *args)
    return general_body(*args)


def solution(mesh):
    in_specs = (
        P(("blk", "ctx"), "tp"),
        P(("blk", "ctx"), "tp"),
        P(("blk", "ctx"), "tp"),
        P(("blk", "ctx"), "tp"),
        P("tp", ("blk", "ctx"), None),
    )
    out_specs = (
        P(("blk", "ctx"), "tp"),
        P(("blk", "ctx"), "tp"),
        P(("blk", "ctx"), "tp"),
        P("tp", ("blk", "ctx"), None),
    )
    return jax.shard_map(
        functools.partial(body, mesh), mesh=mesh, in_specs=in_specs, out_specs=out_specs, check_vma=False
    )
```
